128 devices in a mesh: ctx: 64 (over z_hi, y, x, core), tp: 2 (over z_lo).
Axes of the slice: x: 4, y: 4, z: 4 (z_hi: 2, z_lo: 2; z = z_hi * 2 + z_lo), core: 2. Of those that a mesh axis runs over, the one named last changes fastest.
Arguments:
- queries: bfloat16 [8192, 4096], P('ctx', 'tp'), may hold values from -140 to 140
- rotated_keys: bfloat16 [8192, 256], P('ctx', 'tp'), may hold values from -4.5 to 4.5
- value_matrix: bfloat16 [8192, 256], P('ctx', 'tp'), may hold values from -5 to 5
- lengths: int32 [8], replicated, may hold values from 1 to 4096, 8192 in all
- out_weight: bfloat16 [4096, 4096], P(('tp', 'ctx')), may hold values from -0.09375 to 0.09375
- residual: bfloat16 [8192, 4096], P(('ctx', 'tp')), may hold values from -3 to 3
- expert_ids: int32 [8192, 8], P(('ctx', 'tp')), may hold values from 0 to 127, all different within a row; in each aligned block of 64 rows (0 to 63, 64 to 127, ...) at most 6 rows name the same one
- router_gates: float32 [8192, 8], P(('ctx', 'tp')), may hold values from 0.02 to 0.25
- gate_proj: bfloat16 [128, 4096, 768], P(('ctx', 'tp')), may hold values from -0.09375 to 0.09375
- up_proj: bfloat16 [128, 4096, 768], P(('ctx', 'tp')), may hold values from -0.09375 to 0.09375
- down_proj: bfloat16 [128, 768, 4096], P(('ctx', 'tp')), may hold values from -0.21875 to 0.21875
Outputs:
- layer_out: bfloat16 [8192, 4096], P(('ctx', 'tp'))
The draws below stay inside these ranges and needn't reach their ends.
Inputs may be any that keep to these rules, and one draw needn't show every extreme that they name: The lengths sum to 8192; the largest is half of 8192. `expert_ids`: each row names 8 different experts; in the rows of one device no expert is named by more than 6 rows, and in some device's rows one expert is named by exactly 6.
All inputs are finite; a program needn't handle non-finite values.
Results may differ from the reference program's by a relative error of at most 0.015.
Values may be sent and summed in bfloat16 or wider, within the bound.
No kernel may reach another device: no remote copies, remote signals or barrier semaphores. Data moves between devices by JAX's collectives and lax.ppermute only.
A program may use at most 128 MiB of HBM per device.

```python
import math
import jax
import jax.numpy as jnp
import numpy as np
from jax import lax

D = 4096
HEAD_SIZE = 128
QUERY_HEAD_COUNT = 32
KEY_VALUE_HEADS = 2
FF = 768
TOP = 8
ROLLS = 8
TOK_DEV = 128
TOKEN_COUNT = 8192
EXPERTS = 128
CAP = 6
N_TP = 2


def base_keys(key):
    shared_heads = jax.random.fold_in(key, 11)
    return jnp.clip(jax.random.normal(shared_heads, (TOKEN_COUNT, KEY_VALUE_HEADS * HEAD_SIZE), jnp.float32), -4.5, 4.5)


def draw_rotated_keys(key, part):
    drawn = base_keys(key)
    return drawn.astype(jnp.bfloat16)


def draw_queries(key, part):
    key = jax.random.fold_in(key, 1)
    drawn = jnp.clip(2.5 * jax.random.normal(key, (TOKEN_COUNT, QUERY_HEAD_COUNT * HEAD_SIZE), jnp.float32), -15.0, 15.0)
    return drawn.astype(jnp.bfloat16)


def shard_levels(rng, shape, split, smallest, top_value):
    level = 1.0
    for position, shards_of in split:
        steps = jax.random.uniform(jax.random.fold_in(jax.random.fold_in(rng, 6), position), (shards_of,), jnp.float32, smallest / len(split), top_value / len(split))
        level = level * jnp.repeat(jnp.exp(steps), shape[position] // shards_of).reshape((-1,) + (1,) * (len(shape) - 1 - position))
    return level


def length_profile(count, total, reach, slope):
    weights = [(1 << 20) // math.isqrt(grade ** slope) + 1 for grade in range(2, count + 1)]
    surplus, counts = total - reach - (count - 1), [1] * (count - 1)
    while surplus > 0:
        movable = [i for i in range(count - 1) if counts[i] < reach]
        mass, left = sum([weights[i] for i in movable]), surplus
        for i in movable:
            extra = min(reach - counts[i], max(1, left * weights[i] // mass), surplus)
            counts[i] = counts[i] + extra
            surplus = surplus - extra
    return np.array([reach] + counts)


def ragged(own_key, amount, total, most, slope):
    if amount == 2:
        one = jax.random.randint(own_key, (), max(1, total - most), min(most, total - 1) + 1)
        return jnp.stack([one, total - one])
    tallies = jnp.asarray(length_profile(amount, total, most, slope), jnp.int32)
    couples = (amount - 1) // 2
    giver, receiver = tallies[1:1 + 2 * couples:2], tallies[2:2 + 2 * couples:2]
    slack = jnp.minimum(giver - 1, most - receiver)
    passed = jax.random.randint(jax.random.fold_in(own_key, 1), (couples,), 0, 1 << 20) % (slack + 1)
    tallies = tallies.at[1:1 + 2 * couples:2].set(giver - passed).at[2:2 + 2 * couples:2].set(receiver + passed)
    return tallies[jax.random.permutation(jax.random.fold_in(own_key, 2), amount)]


def routed_block(key, own, number, rows, number_of, top, bound, slope):
    order = jax.random.permutation(key, number_of)
    crowded, usual = portions_of(number_of, rows * top, bound, slope, True), portions_of(number_of, rows * top, bound, slope, False)
    places = jnp.arange(number_of)

    def named(sizes, turn):
        used = int((sizes > 0).sum())
        fixed = max(1, used // 4)
        passed = fixed + (places - fixed + turn * (used - fixed)) % max(1, number_of - fixed)
        return jnp.zeros((number_of,), jnp.int32).at[order[jnp.where(places < fixed, places, passed)]].set(jnp.asarray(sizes, jnp.int32))

    sizes = jnp.where(number % 4 == 0, named(crowded, number // 4), named(usual, number - number // 4 - 1))
    mixed = jax.random.permutation(jax.random.fold_in(own, 3), number_of)
    giver, sink = mixed[0:number_of // 2 * 2:2], mixed[1:number_of // 2 * 2:2]
    room = jnp.minimum(sizes[giver] - 1, bound - sizes[sink]) // 2
    room = jnp.where((giver == order[0]) | (sink == order[0]) | (sizes[sink] == 0), 0, jnp.maximum(room, 0))
    passed = jax.random.randint(jax.random.fold_in(own, 4), (number_of // 2,), 0, 1 << 20) % (room + 1)
    sizes = sizes.at[giver].add(-passed).at[sink].add(passed)
    items = jnp.searchsorted(jnp.cumsum(sizes), jnp.arange(rows * top), side="right").astype(jnp.int32)
    listing = items.reshape(top, rows).T
    listing = listing[jax.random.permutation(jax.random.fold_in(own, 1), rows)]
    turn = jax.random.randint(jax.random.fold_in(own, 2), (rows, 1), 0, top)
    return jnp.take_along_axis(listing, (jnp.arange(top)[None, :] + turn) % top, axis=1)


def portions_of(amount, total, reach, skew, full):
    loads = [(1 << 20) // math.isqrt(standing ** skew) + 1 for standing in range(1, amount + 1)]
    largest = reach if full else min(reach, max(-(-total // amount), total * loads[0] // sum(loads)))
    least = 1 if total - largest >= amount - 1 else 0
    given, rest = [largest] + [least] * (amount - 1), total - largest - least * (amount - 1)
    while rest > 0:
        movable = [i for i in range(1, amount) if given[i] < largest] or [i for i in range(1, amount) if given[i] < reach]
        pool, remaining = sum([loads[i] for i in movable]), rest
        for i in movable:
            more = min(reach - given[i], max(1, remaining * loads[i] // pool), rest)
            given[i] = given[i] + more
            rest = rest - more
    return np.array(given)


def normal_values(key, dims, width, bound, pieces=(), held_as=jnp.bfloat16):
    values = width * jax.random.normal(key, dims, jnp.float32)
    if pieces:
        values = values * shard_levels(key, dims, pieces, -0.22, 0.18)
    return jnp.clip(values, -bound, bound).astype(held_as)


def setup_inputs(seed: int = 0) -> dict:
    seeds = jax.random.split(jax.random.key(seed), 12)
    queries = draw_queries(jax.random.fold_in(seeds[11], 71), 0)
    rotated_keys = draw_rotated_keys(jax.random.fold_in(seeds[11], 71), 0)
    value_matrix = normal_values(seeds[2], (TOKEN_COUNT, KEY_VALUE_HEADS * HEAD_SIZE), 1.0, 5.0, ((0, 64), (1, 2)))
    lengths = ragged(seeds[3], ROLLS, TOKEN_COUNT, TOKEN_COUNT // 2, 2).astype(jnp.int32)
    out_weight = normal_values(seeds[4], (QUERY_HEAD_COUNT * HEAD_SIZE, D), (QUERY_HEAD_COUNT * HEAD_SIZE) ** -0.5, 0.09375, ((0, 128),))
    residual = normal_values(seeds[5], (TOKEN_COUNT, D), 0.5, 3.0, ((0, 128),))
    expert_ids_keys = jax.random.split(jax.random.fold_in(seeds[6], 1), TOKEN_COUNT // (TOK_DEV // N_TP))
    expert_ids_turns = jax.random.permutation(jax.random.fold_in(seeds[6], 3), TOKEN_COUNT // (TOK_DEV // N_TP))
    expert_ids = jax.vmap(lambda own, number: routed_block(jax.random.fold_in(seeds[6], 2), own, number, TOK_DEV // N_TP, EXPERTS, TOP, CAP, 2))(expert_ids_keys, expert_ids_turns).reshape((TOKEN_COUNT, TOP))
    router_gates = jnp.clip(0.02 + 0.23 * jax.random.uniform(seeds[7], (TOKEN_COUNT, TOP), jnp.float32) ** shard_levels(seeds[7], (TOKEN_COUNT, TOP), ((0, 128),), -0.2, 0.2), 0.02, 0.25)
    gate_proj = normal_values(seeds[8], (EXPERTS, D, FF), D ** -0.5, 0.09375, ((0, 128),))
    up_proj = normal_values(seeds[9], (EXPERTS, D, FF), D ** -0.5, 0.09375, ((0, 128),))
    down_proj = normal_values(seeds[10], (EXPERTS, FF, D), FF ** -0.5, 0.21875, ((0, 128),))
    return {"queries": queries, "rotated_keys": rotated_keys, "value_matrix": value_matrix, "lengths": lengths, "out_weight": out_weight, "residual": residual, "expert_ids": expert_ids, "router_gates": router_gates, "gate_proj": gate_proj, "up_proj": up_proj, "down_proj": down_proj}


def rollout_of(lengths, positions):
    ends = jnp.cumsum(lengths).astype(jnp.int32)
    return lax.optimization_barrier(jnp.sum((positions[:, None] >= ends[None, :]).astype(jnp.int32), axis=1)).astype(jnp.int32)

def attention(queries, rotated_keys, value_matrix, lengths):
    query_group = QUERY_HEAD_COUNT // KEY_VALUE_HEADS
    positions = jnp.arange(TOKEN_COUNT, dtype=jnp.int32)
    rollout = rollout_of(lengths, positions)
    widened_keys = rotated_keys.astype(jnp.float32).reshape(TOKEN_COUNT, KEY_VALUE_HEADS, HEAD_SIZE)
    widened_values = value_matrix.astype(jnp.float32).reshape(TOKEN_COUNT, KEY_VALUE_HEADS, HEAD_SIZE)
    feature_width = math.gcd(TOKEN_COUNT, 256)
    scale = 1.0 / math.sqrt(HEAD_SIZE)

    def one_block(number):
        begin = (number * feature_width).astype(jnp.int32)
        picked_rows = lax.dynamic_slice_in_dim(queries, begin, feature_width, 0).astype(jnp.float32)
        picked_rows = picked_rows.reshape(feature_width, KEY_VALUE_HEADS, query_group, HEAD_SIZE)
        scores = jnp.einsum('tgjd,sgd->gjts', picked_rows, widened_keys) * scale
        query_pos = lax.dynamic_slice_in_dim(positions, begin, feature_width, 0)
        query_roll = lax.dynamic_slice_in_dim(rollout, begin, feature_width, 0)
        allowed = (positions[None, :] <= query_pos[:, None]) & (rollout[None, :] == query_roll[:, None])
        scores = jnp.where(allowed[None, None], scores, -jnp.inf)
        highest = lax.optimization_barrier(jnp.max(scores, axis=-1, keepdims=True))
        expo = jnp.exp(scores - highest)
        total = lax.optimization_barrier(jnp.sum(expo, axis=-1))
        rounded = lax.optimization_barrier(expo.astype(jnp.bfloat16))
        weights = rounded.astype(jnp.float32)
        mixed = jnp.einsum('gjts,sgd->tgjd', weights, widened_values)
        mixed = mixed / jnp.transpose(total, (2, 0, 1))[..., None]
        return mixed.reshape(feature_width, QUERY_HEAD_COUNT * HEAD_SIZE).astype(jnp.bfloat16)
    blocks = lax.map(one_block, jnp.arange(TOKEN_COUNT // feature_width, dtype=jnp.int32))
    return blocks.reshape(TOKEN_COUNT, QUERY_HEAD_COUNT * HEAD_SIZE)

def expert_layer(normed, expert_ids, router_gates, gate_proj, up_proj, down_proj):
    per_block = TOK_DEV // N_TP
    blocks = TOKEN_COUNT // per_block
    flat_ids = expert_ids.reshape(blocks, per_block * TOP)
    onehot = (flat_ids[:, :, None] == jnp.arange(EXPERTS, dtype=jnp.int32)[None, None, :]).astype(jnp.int32)
    earlier = (jnp.cumsum(onehot, axis=1) - onehot).astype(jnp.int32)
    slot_index = lax.optimization_barrier(jnp.sum(earlier * onehot, axis=2)).astype(jnp.int32)
    token_row = (jnp.arange(blocks, dtype=jnp.int32)[:, None] * per_block + jnp.arange(per_block * TOP, dtype=jnp.int32)[None, :] // TOP).astype(jnp.int32)
    block_index = jnp.broadcast_to(jnp.arange(blocks, dtype=jnp.int32)[:, None], (blocks, per_block * TOP))
    table = jnp.full((EXPERTS, blocks, CAP), TOKEN_COUNT, jnp.int32).at[flat_ids, block_index, slot_index].set(token_row)
    gate_table = jnp.zeros((EXPERTS, blocks, CAP), router_gates.dtype).at[flat_ids, block_index, slot_index].set(router_gates.reshape(blocks, per_block * TOP))
    padded = jnp.concatenate([normed, jnp.zeros((1, D), normed.dtype)], axis=0)

    def one_expert(summed, inputs):
        rows_used, gate_used, gate_mat, up_mat, down_mat = inputs
        flat_rows = rows_used.reshape(blocks * CAP)
        chosen = padded[flat_rows]
        gate = jnp.dot(chosen, gate_mat, preferred_element_type=jnp.float32)
        upward = jnp.dot(chosen, up_mat, preferred_element_type=jnp.float32)
        hidden = (jax.nn.silu(gate) * upward).astype(jnp.bfloat16)
        produced = jnp.dot(hidden, down_mat, preferred_element_type=jnp.float32).astype(jnp.bfloat16)
        scaled = produced.astype(jnp.float32) * gate_used.reshape(blocks * CAP, 1)
        return (summed.at[flat_rows].add(scaled), None)
    start_sum = jnp.zeros((TOKEN_COUNT + 1, D), jnp.float32)
    summed, unused = lax.scan(one_expert, start_sum, (table, gate_table, gate_proj, up_proj, down_proj))
    return summed[:TOKEN_COUNT]

def reference(queries, rotated_keys, value_matrix, lengths, out_weight, residual, expert_ids, router_gates, gate_proj, up_proj, down_proj):
    attended = attention(queries, rotated_keys, value_matrix, lengths)
    projected = jnp.dot(attended, out_weight, preferred_element_type=jnp.float32)
    hidden_state = (residual.astype(jnp.float32) + projected).astype(jnp.bfloat16)
    widened = hidden_state.astype(jnp.float32)
    normed = (widened * lax.rsqrt(lax.optimization_barrier(jnp.mean(widened * widened, axis=1, keepdims=True)) + 1e-06)).astype(jnp.bfloat16)
    mixed = expert_layer(normed, expert_ids, router_gates, gate_proj, up_proj, down_proj)
    return (widened + mixed).astype(jnp.bfloat16)
```

```python
import math

import jax
import jax.numpy as jnp
from jax import lax
from jax.experimental import pallas as pl
from jax.experimental.pallas import tpu as pltpu
from jax.sharding import Mesh
from jax.sharding import PartitionSpec as P

HEAD = 128
CAP = 6
ROWS = 64
GROUP = 8
SLOTS = GROUP * CAP
CHUNK = 512
NEG = -1e30
BF16 = jnp.bfloat16
F32 = jnp.float32
AXES = ("zh", "y", "x", "c", "zl")
LINE = ("zh", "c", "zl")
Z = ("zh", "zl")


def rotated(count, step):
    return [(i, (i + step) % count) for i in range(count)]


def flipped(count, bits):
    return [(i, i ^ bits) for i in range(count)]


def attention_kernel(lim, low, high, order, q, kv, kpos, qpos, qstart, out, best, accum):
    scale = math.log2(math.e) / math.sqrt(HEAD)
    heads = q.shape[1] // HEAD
    tokens = q.shape[0]
    best[...] = jnp.full(best.shape, NEG, F32)
    accum[...] = jnp.zeros(accum.shape, F32)

    def update(number, masked):
        begin = pl.multiple_of(number * CHUNK, CHUNK)
        keys = kv[pl.ds(begin, CHUNK), :HEAD]
        values = kv[pl.ds(begin, CHUNK), HEAD:]
        values = jnp.concatenate([values, jnp.ones((CHUNK, HEAD), BF16)], axis=1)
        if masked:
            at = kpos[number]
            allowed = (at <= qpos[...]) & (at >= qstart[...])
        for head in range(heads):
            rows = pl.ds(head * tokens, tokens)
            scores = lax.dot_general(
                q[:, head * HEAD : (head + 1) * HEAD],
                keys,
                (((1,), (1,)), ((), ())),
                preferred_element_type=F32,
            )
            if masked:
                scores = jnp.where(allowed, scores, NEG)
            old = best[rows, :]
            new = jnp.maximum(old, jnp.max(scores, axis=1, keepdims=True))
            factor = jnp.exp2((old - new) * scale)
            expo = jnp.exp2((scores - jnp.concatenate([new] * (CHUNK // HEAD), axis=1)) * scale)
            added = jnp.dot(expo.astype(BF16), values, preferred_element_type=F32)
            accum[rows, :] = accum[rows, :] * jnp.concatenate([factor, factor], axis=1) + added
            best[rows, :] = new

    def step(i, carry):
        number = order[i]
        used = (low[number] <= lim[1]) & (high[number] >= lim[2])
        whole = (high[number] <= lim[0]) & (low[number] >= lim[3])

        @pl.when(used & whole)
        def _():
            update(number, False)

        @pl.when(used & jnp.logical_not(whole))
        def _():
            update(number, True)

        return carry

    lax.fori_loop(0, order.shape[0], step, 0)
    for head in range(heads):
        rows = pl.ds(head * tokens, tokens)
        state = accum[rows, :]
        out[:, head * HEAD : (head + 1) * HEAD] = (state[:, :HEAD] / state[:, HEAD:]).astype(BF16)


def attend(queries, kv, key_pos, low, high, order, query_pos, query_start):
    tokens, width = queries.shape
    heads_a_step = 4
    lim = jnp.stack(
        [query_pos[0], query_pos[-1], jnp.min(query_start), jnp.max(query_start)]
    ).astype(jnp.int32)
    smem = pl.BlockSpec(memory_space=pltpu.SMEM)
    cols = heads_a_step * HEAD
    return pl.pallas_call(
        attention_kernel,
        grid=(width // cols,),
        in_specs=[
            smem,
            smem,
            smem,
            smem,
            pl.BlockSpec((tokens, cols), lambda i: (0, i)),
            pl.BlockSpec(kv.shape, lambda i: (0, 0)),
            pl.BlockSpec(key_pos.shape, lambda i: (0, 0, 0)),
            pl.BlockSpec((tokens, 1), lambda i: (0, 0)),
            pl.BlockSpec((tokens, 1), lambda i: (0, 0)),
        ],
        out_specs=pl.BlockSpec((tokens, cols), lambda i: (0, i)),
        out_shape=jax.ShapeDtypeStruct((tokens, width), BF16),
        scratch_shapes=[
            pltpu.VMEM((heads_a_step * tokens, HEAD), F32),
            pltpu.VMEM((heads_a_step * tokens, 2 * HEAD), F32),
        ],
        compiler_params=pltpu.CompilerParams(vmem_limit_bytes=40 << 20),
        name="attention",
    )(lim, low, high, order, queries, kv, key_pos, query_pos[:, None], query_start[:, None])


def projection_kernel(slot, parts, weight, residual, hidden, accum):
    step = pl.program_id(0)

    @pl.when(step == 0)
    def _():
        accum[...] = residual[...].astype(F32)

    total = accum[...]
    for half in range(2):
        left = jnp.concatenate([parts[slot[2 * block + half]] for block in range(4)], axis=0)
        total = total + jnp.dot(left, weight[half], preferred_element_type=F32)
    accum[...] = total

    @pl.when(step == pl.num_programs(0) - 1)
    def _():
        hidden[...] = total.astype(BF16)


def project(slot, parts, weight, residual):
    steps = 4
    depth = weight.shape[1] // steps
    tokens, width = residual.shape
    return pl.pallas_call(
        projection_kernel,
        grid=(steps,),
        in_specs=[
            pl.BlockSpec(memory_space=pltpu.SMEM),
            pl.BlockSpec((8, parts.shape[1], depth), lambda k: (0, 0, k)),
            pl.BlockSpec((2, depth, width), lambda k: (0, k, 0)),
            pl.BlockSpec((tokens, width), lambda k: (0, 0)),
        ],
        out_specs=pl.BlockSpec((tokens, width), lambda k: (0, 0)),
        out_shape=jax.ShapeDtypeStruct((tokens, width), BF16),
        scratch_shapes=[pltpu.VMEM((tokens, width), F32)],
        compiler_params=pltpu.CompilerParams(vmem_limit_bytes=40 << 20),
        name="projection",
    )(slot, parts, weight, residual)


def slots_of(ids, experts):
    tokens = ids.shape[1]
    expert = lax.broadcasted_iota(jnp.int32, (experts, tokens), 0)
    named = jnp.zeros((experts, tokens), F32)
    for k in range(ids.shape[0]):
        named = named + jnp.where(ids[k : k + 1, :] == expert, 1.0, 0.0)
    first = lax.broadcasted_iota(jnp.int32, (tokens, tokens), 0)
    second = lax.broadcasted_iota(jnp.int32, (tokens, tokens), 1)
    before = (first < second) & (first // ROWS == second // ROWS)
    rank = jnp.dot(
        named.astype(BF16), jnp.where(before, 1.0, 0.0).astype(BF16), preferred_element_type=F32
    )
    block = lax.broadcasted_iota(jnp.int32, (experts, tokens), 1) // ROWS
    return jnp.where(named > 0, rank + (block * CAP).astype(F32), -1.0)


def dispatch_kernel(ids, hidden, out, slots):
    step = pl.program_id(0)
    tokens = hidden.shape[0]
    count = out.shape[0]

    @pl.when(step == 0)
    def _():
        slots[...] = slots_of(ids[...], slots.shape[0])

    row = lax.broadcasted_iota(jnp.int32, (SLOTS, tokens), 0).astype(F32)
    mine = slots[pl.ds(pl.multiple_of(step * count, count), count), :]
    picks = [jnp.where(mine[e : e + 1, :] == row, 1.0, 0.0).astype(BF16) for e in range(count)]
    rows = jnp.dot(jnp.concatenate(picks, axis=0), hidden[...], preferred_element_type=F32)
    out[...] = rows.astype(BF16).reshape(out.shape)


def dispatch(ids, hidden, experts):
    tokens, width = hidden.shape
    count = 8
    return pl.pallas_call(
        dispatch_kernel,
        grid=(experts // count,),
        in_specs=[
            pl.BlockSpec(ids.shape, lambda i: (0, 0)),
            pl.BlockSpec((tokens, width), lambda i: (0, 0)),
        ],
        out_specs=pl.BlockSpec((count, SLOTS, width), lambda i: (i, 0, 0)),
        out_shape=jax.ShapeDtypeStruct((experts, SLOTS, width), BF16),
        scratch_shapes=[pltpu.VMEM((experts, tokens), F32)],
        compiler_params=pltpu.CompilerParams(vmem_limit_bytes=40 << 20),
        name="dispatch",
    )(ids, hidden)


def expert_kernel(rows, gate_w, up_w, down_w, out, gate, up, squares, act):
    step = pl.program_id(0)
    half = pl.num_programs(0) // 2
    width = rows.shape[-1]
    count = act.shape[0]

    @pl.when(step == 0)
    def _():
        gate[...] = jnp.zeros(gate.shape, F32)
        up[...] = jnp.zeros(up.shape, F32)
        squares[...] = jnp.zeros(squares.shape, F32)

    @pl.when(step < half)
    def _():
        block = rows[...].reshape(count, width)
        gate[...] += jnp.dot(block, gate_w[0], preferred_element_type=F32)
        up[...] += jnp.dot(block, up_w[0], preferred_element_type=F32)
        wide = block.astype(F32)
        wide = wide * wide
        total = wide[:, :HEAD]
        for i in range(1, width // HEAD):
            total = total + wide[:, i * HEAD : (i + 1) * HEAD]
        squares[...] += total

    @pl.when(step == half - 1)
    def _():
        mean = jnp.sum(squares[...], axis=1, keepdims=True) / (width * half)
        factor = lax.rsqrt(mean + 1e-06)
        value = gate[...] * factor
        act[...] = (value / (1.0 + jnp.exp(-value)) * (up[...] * factor)).astype(BF16)

    @pl.when(step >= half)
    def _():
        result = jnp.dot(act[...], down_w[0], preferred_element_type=F32)
        out[...] = result.astype(BF16).reshape(out.shape)


def expert(rows, gate_w, up_w, down_w):
    high, groups, low, slots, width = rows.shape
    steps = high * low
    hidden_units = gate_w.shape[2]
    count = groups * slots
    last = steps - 1

    def first(i):
        return jnp.minimum(i, last)

    def second(i):
        return jnp.maximum(i - steps, 0)

    return pl.pallas_call(
        expert_kernel,
        grid=(2 * steps,),
        in_specs=[
            pl.BlockSpec(
                (1, groups, 1, slots, width),
                lambda i: (first(i) // low, 0, lax.rem(first(i), low), 0, 0),
            ),
            pl.BlockSpec((1, width, hidden_units), lambda i: (0, first(i), 0)),
            pl.BlockSpec((1, width, hidden_units), lambda i: (0, first(i), 0)),
            pl.BlockSpec((1, hidden_units, width), lambda i: (0, 0, second(i))),
        ],
        out_specs=pl.BlockSpec(
            (1, groups, 1, slots, width),
            lambda i: (second(i) // low, 0, lax.rem(second(i), low), 0, 0),
        ),
        out_shape=jax.ShapeDtypeStruct(rows.shape, BF16),
        scratch_shapes=[
            pltpu.VMEM((count, hidden_units), F32),
            pltpu.VMEM((count, hidden_units), F32),
            pltpu.VMEM((count, HEAD), F32),
            pltpu.VMEM((count, hidden_units), BF16),
        ],
        compiler_params=pltpu.CompilerParams(vmem_limit_bytes=48 << 20),
        name="expert",
    )(rows, gate_w, up_w, down_w)


def combine_kernel(ids, gates, answers, hidden, out, slots, weights, accum):
    step = pl.program_id(0)
    tokens = hidden.shape[0]
    count = answers.shape[0]
    experts = slots.shape[0]

    @pl.when(step == 0)
    def _():
        slots[...] = slots_of(ids[...], experts)
        number = lax.broadcasted_iota(jnp.int32, (experts, tokens), 0)
        total = jnp.zeros((experts, tokens), F32)
        for k in range(ids.shape[0]):
            total = total + jnp.where(ids[k : k + 1, :] == number, gates[k : k + 1, :], 0.0)
        weights[...] = total
        accum[...] = hidden[...].astype(F32)

    row = lax.broadcasted_iota(jnp.int32, (SLOTS, tokens), 0).astype(F32)
    begin = pl.ds(pl.multiple_of(step * count, count), count)
    mine, scale = slots[begin, :], weights[begin, :]
    picks = [
        jnp.where(mine[e : e + 1, :] == row, scale[e : e + 1, :], 0.0).astype(BF16)
        for e in range(count)
    ]
    total = accum[...] + lax.dot_general(
        jnp.concatenate(picks, axis=0),
        answers[...].reshape(count * SLOTS, answers.shape[2]),
        (((0,), (0,)), ((), ())),
        preferred_element_type=F32,
    )
    accum[...] = total

    @pl.when(step == pl.num_programs(0) - 1)
    def _():
        out[...] = total.astype(BF16)


def combine(ids, gates, answers, hidden):
    tokens, width = hidden.shape
    experts = answers.shape[0]
    count = 8
    return pl.pallas_call(
        combine_kernel,
        grid=(experts // count,),
        in_specs=[
            pl.BlockSpec(ids.shape, lambda i: (0, 0)),
            pl.BlockSpec(gates.shape, lambda i: (0, 0)),
            pl.BlockSpec((count, SLOTS, width), lambda i: (i, 0, 0)),
            pl.BlockSpec((tokens, width), lambda i: (0, 0)),
        ],
        out_specs=pl.BlockSpec((tokens, width), lambda i: (0, 0)),
        out_shape=jax.ShapeDtypeStruct((tokens, width), BF16),
        scratch_shapes=[
            pltpu.VMEM((experts, tokens), F32),
            pltpu.VMEM((experts, tokens), F32),
            pltpu.VMEM((tokens, width), F32),
        ],
        compiler_params=pltpu.CompilerParams(vmem_limit_bytes=40 << 20),
        name="combine",
    )(ids, gates, answers, hidden)


def gather_kv(rotated_keys, value_matrix):
    own = jnp.concatenate([rotated_keys, value_matrix], axis=1)
    tokens = own.shape[0]
    row = jnp.stack([own] + [lax.ppermute(own, "x", rotated(4, k)) for k in range(1, 4)])
    row_other = lax.ppermute(row, "c", flipped(2, 1))
    rest = jnp.concatenate([lax.ppermute(row, ("zh", "y"), rotated(8, k)) for k in range(1, 5)])
    rest_other = lax.ppermute(rest, "c", flipped(2, 1))
    kv = jnp.concatenate([row, row_other, rest, rest_other]).reshape(-1, own.shape[1])
    slab = lax.axis_index(("zh", "y"))
    core = lax.axis_index("c")
    place = (lax.axis_index("x") - jnp.arange(4, dtype=jnp.int32)) % 4
    back = jnp.array([0, 0, 1, 2, 3, 4, 1, 2, 3, 4], jnp.int32)
    side = jnp.array([0, 1, 0, 0, 0, 0, 1, 1, 1, 1], jnp.int32)
    begin = ((slab - back) % 8) * 8 * tokens + (core ^ side) * tokens
    pos = begin[:, None, None] + (place * 2 * tokens)[None, :, None]
    pos = pos + jnp.arange(tokens, dtype=jnp.int32)[None, None, :]
    low = begin.astype(jnp.int32)
    high = (begin + 7 * tokens - 1).astype(jnp.int32)
    return kv, pos.astype(jnp.int32).reshape(10, 1, 4 * tokens), low, high


def gather_attended(own):
    near = lax.ppermute(own, Z, flipped(4, 1))
    far = lax.ppermute(own, Z, flipped(4, 3))
    cut = own.shape[0] // 2
    opposite = jnp.concatenate(
        [
            lax.ppermute(near[:cut], Z, flipped(4, 3)),
            lax.ppermute(far[cut:], Z, flipped(4, 1)),
        ]
    )
    mine = jnp.stack([own, near, opposite, far])
    other = lax.ppermute(mine, "c", flipped(2, 1))
    z, core = lax.axis_index(Z), lax.axis_index("c")
    slot = []
    for zh in range(2):
        for c in range(2):
            for half in range(2):
                slot.append((core ^ c) * 4 + (z ^ (zh * 2 + half)))
    return jnp.concatenate([mine, other]), jnp.stack(slot).astype(jnp.int32)


def body(
    queries,
    rotated_keys,
    value_matrix,
    lengths,
    out_weight,
    residual,
    expert_ids,
    router_gates,
    gate_proj,
    up_proj,
    down_proj,
):
    tokens = queries.shape[0]
    own_rows, model_width = residual.shape
    experts = 2 * 4 * 4 * 2 * 2
    width = model_width // GROUP

    kv, key_pos, low, high = gather_kv(rotated_keys, value_matrix)

    weight_rows = out_weight.shape[0]
    meta = jnp.concatenate([expert_ids.astype(BF16), router_gates.astype(BF16)], axis=1)
    meta = meta.reshape(-1, width)
    used = meta.shape[0]
    meta = jnp.pad(meta, ((0, 16 - used), (0, 0)))
    sent = jnp.concatenate(
        [
            out_weight.reshape(weight_rows, GROUP, width).transpose(1, 0, 2),
            residual.reshape(own_rows, GROUP, width).transpose(1, 0, 2),
            jnp.broadcast_to(meta[None], (GROUP, 16, width)),
        ],
        axis=1,
    )
    got = lax.all_to_all(sent, LINE, split_axis=0, concat_axis=0, tiled=True)
    weight_part = got[:, :weight_rows].reshape(GROUP * weight_rows, width)
    line_residual = got[:, weight_rows : weight_rows + own_rows].reshape(GROUP * own_rows, width)
    meta = got[:, weight_rows + own_rows : weight_rows + own_rows + used]
    meta = meta.reshape(GROUP * own_rows, 16).T
    ids = meta[:8].astype(jnp.int32)
    gates = meta[8:].astype(F32)

    weight = lax.all_gather(weight_part, ("y", "x"), axis=0, tiled=True)
    weight = weight.reshape(16, 2, 2, 2, weight_rows, width).transpose(3, 1, 0, 2, 4, 5)
    weight = weight.reshape(2, model_width // 2, width)

    query_pos = lax.axis_index(("zh", "y", "x", "c")) * tokens + jnp.arange(tokens, dtype=jnp.int32)
    starts = jnp.cumsum(lengths) - lengths
    query_start = jnp.max(
        jnp.where(starts[None, :] <= query_pos[:, None], starts[None, :], 0), axis=1
    ).astype(jnp.int32)
    order = jnp.array([0, 1, 2, 6, 3, 7, 4, 8, 5, 9], jnp.int32)
    attended = attend(queries, kv, key_pos, low, high, order, query_pos, query_start)

    parts, slot = gather_attended(attended)
    hidden = project(slot, parts, weight, line_residual)

    outgoing = dispatch(ids, hidden, experts)
    incoming = lax.all_to_all(outgoing, AXES, split_axis=0, concat_axis=0, tiled=True)
    produced = expert(
        incoming.reshape(2, 16, 4, SLOTS, width), gate_proj, up_proj, down_proj
    ).reshape(experts, SLOTS, width)
    answers = lax.all_to_all(produced, AXES, split_axis=0, concat_axis=0, tiled=True)
    mixed = combine(ids, gates, answers, hidden)
    final = lax.all_to_all(
        mixed.reshape(GROUP, own_rows, width), LINE, split_axis=0, concat_axis=0, tiled=True
    )
    return final.transpose(1, 0, 2).reshape(own_rows, model_width)


def solution(mesh):
    fine = Mesh(mesh.devices.reshape(2, 4, 4, 2, 2), AXES)
    ctx = ("zh", "y", "x", "c")
    both = P(AXES, None)
    in_specs = (
        P(ctx, "zl"),
        P(ctx, "zl"),
        P(ctx, "zl"),
        P(),
        P(("zl",) + ctx, None),
        both,
        both,
        both,
        P(AXES, None, None),
        P(AXES, None, None),
        P(AXES, None, None),
    )
    return jax.shard_map(body, mesh=fine, in_specs=in_specs, out_specs=both, check_vma=False)
```

```python
import functools
import math

import jax
import jax.numpy as jnp
from jax import lax
from jax.experimental import pallas as pl
from jax.experimental.pallas import tpu as pltpu
from jax.sharding import Mesh
from jax.sharding import PartitionSpec as P

HEAD = 128
CAP = 6
ROWS = 64
GROUP = 8
SLOTS = GROUP * CAP
CHUNK = 512
EDGE = 640
FIRST, SECOND = 4, 2
NEG = -1e30
BF16 = jnp.bfloat16
F32 = jnp.float32
AXES = ("zh", "y", "x", "c", "zl")
LINE = ("zh", "c", "zl")
Z = ("zh", "zl")


def rotated(count, step):
    return [(i, (i + step) % count) for i in range(count)]


def flipped(count, bits):
    return [(i, i ^ bits) for i in range(count)]


def attention_kernel(lim, low, high, q, kv, other, kpos, qpos, qstart, out, best, accum):
    scale = math.log2(math.e) / math.sqrt(HEAD)
    heads = q.shape[1] // HEAD
    tokens = q.shape[0]
    best[...] = jnp.full(best.shape, NEG, F32)
    accum[...] = jnp.zeros(accum.shape, F32)

    def update(source, begin, count, allowed):
        keys = source[pl.ds(begin, count), :HEAD]
        values = source[pl.ds(begin, count), HEAD:]
        values = jnp.concatenate([values, jnp.ones((count, HEAD), BF16)], axis=1)
        for head in range(heads):
            rows = pl.ds(head * tokens, tokens)
            scores = lax.dot_general(
                q[:, head * HEAD : (head + 1) * HEAD],
                keys,
                (((1,), (1,)), ((), ())),
                preferred_element_type=F32,
            )
            if allowed is not None:
                scores = jnp.where(allowed, scores, NEG)
            old = best[rows, :]
            new = jnp.maximum(old, jnp.max(scores, axis=1, keepdims=True))
            factor = jnp.exp2((old - new) * scale)
            expo = jnp.exp2((scores - jnp.concatenate([new] * (count // HEAD), axis=1)) * scale)
            added = jnp.dot(expo.astype(BF16), values, preferred_element_type=F32)
            accum[rows, :] = accum[rows, :] * jnp.concatenate([factor, factor], axis=1) + added
            best[rows, :] = new

    def inside(at):
        return (at <= qpos[...]) & (at >= qstart[...])

    for side, source in enumerate((kv, other)):
        update(source, 0, EDGE, inside(kpos[side, :, :EDGE]))

    full = (kv.shape[0] - EDGE) // CHUNK
    for side, source in enumerate((kv, other)):

        def step(i, carry, side=side, source=source):
            number = side * full + i
            used = (low[number] <= lim[1]) & (high[number] >= lim[2])
            whole = (high[number] <= lim[0]) & (low[number] >= lim[3])
            begin = pl.multiple_of(EDGE + i * CHUNK, HEAD)

            @pl.when(used & whole)
            def _():
                update(source, begin, CHUNK, None)

            @pl.when(used & jnp.logical_not(whole))
            def _():
                at = kpos[side, :, pl.ds(begin, CHUNK)]
                update(source, begin, CHUNK, inside(at))

            return carry

        lax.fori_loop(0, full, step, 0)

    for head in range(heads):
        rows = pl.ds(head * tokens, tokens)
        state = accum[rows, :]
        out[:, head * HEAD : (head + 1) * HEAD] = (state[:, :HEAD] / state[:, HEAD:]).astype(BF16)


def attend(queries, kv, other, key_pos, low, high, lim, query_pos, query_start):
    tokens, width = queries.shape
    smem = pl.BlockSpec(memory_space=pltpu.SMEM)
    vmem = pl.BlockSpec(memory_space=pltpu.VMEM)
    rows = width // HEAD * tokens
    return pl.pallas_call(
        attention_kernel,
        in_specs=[smem] * 3 + [vmem] * 6,
        out_specs=vmem,
        out_shape=jax.ShapeDtypeStruct((tokens, width), BF16),
        scratch_shapes=[pltpu.VMEM((rows, HEAD), F32), pltpu.VMEM((rows, 2 * HEAD), F32)],
        compiler_params=pltpu.CompilerParams(vmem_limit_bytes=32 << 20),
        cost_estimate=pl.CostEstimate(
            flops=10_000_000_000, bytes_accessed=4_000_000, transcendentals=8_000_000
        ),
        name="attention",
    )(lim, low, high, queries, kv, other, key_pos, query_pos, query_start)


def projection_kernel(steps, *refs):
    slot = refs[0]
    weight, residual, slots, hidden, outgoing, accum = refs[21:]
    step = pl.program_id(0)
    blocks, rows_each, width = residual.shape
    tokens = blocks * rows_each
    count = outgoing.shape[0]

    @pl.when(step < steps)
    def _():
        total = None
        for high in range(2):
            own, own_c, near, near_c, far, far_c, first, first_c, second, second_c = refs[
                1 + high : 21 : 2
            ]
            rows = ((own, own_c, first, second, first_c, second_c), (near, near_c, far, far_c))
            for other in range(2):
                pieces = []
                for x in range(4):
                    for core in range(2):
                        pieces.append(weight[0, x, slot[(high * 2 + core) * 2 + other]])
                part = jnp.dot(
                    jnp.concatenate([ref[...] for ref in rows[other]], axis=0),
                    jnp.concatenate(pieces, axis=0),
                    preferred_element_type=F32,
                )
                total = part if total is None else total + part

        @pl.when(step == 0)
        def _():
            accum[...] = total

        @pl.when(step > 0)
        def _():
            accum[...] += total

    @pl.when(step == steps - 1)
    def _():
        share = tokens // 4
        for block in range(4):
            place = slot[8 + block]
            part = accum[block * share : (block + 1) * share, :]
            base = jnp.concatenate([residual[2 * place], residual[2 * place + 1]], axis=0)
            here = pl.ds(pl.multiple_of(place * share, share), share)
            hidden[here, :] = (base.astype(F32) + part).astype(BF16)

    @pl.when(step >= steps)
    def _():
        row = lax.broadcasted_iota(jnp.int32, (SLOTS, tokens), 0).astype(F32)
        mine = slots[...]
        picks = [jnp.where(mine[e : e + 1, :] == row, 1.0, 0.0).astype(BF16) for e in range(count)]
        sent = jnp.dot(jnp.concatenate(picks, axis=0), hidden[...], preferred_element_type=F32)
        outgoing[...] = sent.astype(BF16).reshape(outgoing.shape)


def project(slot, blocks, weight, residual, slots):
    width = residual.shape[2]
    tokens = residual.shape[0] * residual.shape[1]
    experts = slots.shape[0]
    count = 16
    steps = weight.shape[0]
    depth = blocks[0].shape[1] // (2 * steps)

    def early(k):
        return jnp.minimum(k, steps - 1)

    def late(k):
        return jnp.maximum(k - steps, 0)

    specs = []
    for ref in blocks:
        specs.append(pl.BlockSpec((ref.shape[0], depth), lambda k: (0, early(k))))
        specs.append(pl.BlockSpec((ref.shape[0], depth), lambda k: (0, early(k) + steps)))
    return pl.pallas_call(
        functools.partial(projection_kernel, steps),
        grid=(steps + experts // count,),
        in_specs=[pl.BlockSpec(memory_space=pltpu.SMEM)]
        + specs
        + [
            pl.BlockSpec((1,) + weight.shape[1:], lambda k: (early(k), 0, 0, 0, 0)),
            pl.BlockSpec(residual.shape, lambda k: (0, 0, 0)),
            pl.BlockSpec((count, tokens), lambda k: (late(k), 0)),
        ],
        out_specs=(
            pl.BlockSpec((tokens, width), lambda k: (0, 0)),
            pl.BlockSpec((count, SLOTS, width), lambda k: (late(k), 0, 0)),
        ),
        out_shape=(
            jax.ShapeDtypeStruct((tokens, width), BF16),
            jax.ShapeDtypeStruct((experts, SLOTS, width), BF16),
        ),
        scratch_shapes=[pltpu.VMEM((tokens, width), F32)],
        compiler_params=pltpu.CompilerParams(vmem_limit_bytes=36 << 20),
        name="projection",
    )(slot, *[ref for ref in blocks for _ in range(2)], weight, residual, slots)


def slots_of(ids, experts):
    tokens = ids.shape[1]
    expert = lax.broadcasted_iota(jnp.int32, (experts, tokens), 0)
    named = jnp.zeros((experts, tokens), F32)
    for k in range(ids.shape[0]):
        named = named + jnp.where(ids[k : k + 1, :] == expert, 1.0, 0.0)
    first = lax.broadcasted_iota(jnp.int32, (tokens, tokens), 0)
    second = lax.broadcasted_iota(jnp.int32, (tokens, tokens), 1)
    before = (first < second) & (first // ROWS == second // ROWS)
    rank = jnp.dot(
        named.astype(BF16), jnp.where(before, 1.0, 0.0).astype(BF16), preferred_element_type=F32
    )
    block = lax.broadcasted_iota(jnp.int32, (experts, tokens), 1) // ROWS
    return jnp.where(named > 0, rank + (block * CAP).astype(F32), -1.0)


def routing_kernel(ids, gates, slots, weights):
    experts, tokens = slots.shape
    slots[...] = slots_of(ids[...], experts)
    number = lax.broadcasted_iota(jnp.int32, (experts, tokens), 0)
    total = jnp.zeros((experts, tokens), F32)
    for k in range(ids.shape[0]):
        total = total + jnp.where(ids[k : k + 1, :] == number, gates[k : k + 1, :], 0.0)
    weights[...] = total


def route(ids, gates, experts):
    shape = jax.ShapeDtypeStruct((experts, ids.shape[1]), F32)
    return pl.pallas_call(
        routing_kernel,
        out_shape=(shape, shape),
        compiler_params=pltpu.CompilerParams(vmem_limit_bytes=16 << 20),
        name="routing",
    )(ids, gates)


def expert_kernel(rows, gate_w, up_w, down_w, out, gate, up, squares, act):
    step = pl.program_id(0)
    groups, taken, slots, width = rows.shape[1:]
    count = groups * slots
    model_width = gate_w.shape[1] * FIRST

    @pl.when(step < FIRST)
    def _():
        block = jnp.concatenate(
            [rows[0, :, i].reshape(count, width) for i in range(taken)], axis=1
        )
        gate_part = jnp.dot(block, gate_w[0], preferred_element_type=F32)
        up_part = jnp.dot(block, up_w[0], preferred_element_type=F32)
        wide = block.astype(F32)
        wide = wide * wide
        total = wide[:, :HEAD]
        for i in range(1, taken * width // HEAD):
            total = total + wide[:, i * HEAD : (i + 1) * HEAD]

        @pl.when(step == 0)
        def _():
            gate[...] = gate_part
            up[...] = up_part
            squares[...] = total

        @pl.when(step > 0)
        def _():
            gate[...] += gate_part
            up[...] += up_part
            squares[...] += total

    @pl.when(step == FIRST - 1)
    def _():
        mean = jnp.sum(squares[...], axis=1, keepdims=True) / model_width
        factor = lax.rsqrt(mean + 1e-06)
        value = gate[...] * factor
        act[...] = (value / (1.0 + jnp.exp(-value)) * (up[...] * factor)).astype(BF16)

    @pl.when(step >= FIRST)
    def _():
        result = jnp.dot(act[...], down_w[0], preferred_element_type=F32).astype(BF16)
        for i in range(out.shape[2]):
            out[0, :, i] = result[:, i * width : (i + 1) * width].reshape(groups, slots, width)


def expert(rows, gate_w, up_w, down_w):
    high, groups, low, slots, width = rows.shape
    hidden_units = gate_w.shape[2]
    count = groups * slots
    taken, given = high * low // FIRST, high * low // SECOND

    def first(i):
        return jnp.minimum(i, FIRST - 1)

    def second(i):
        return jnp.maximum(i - FIRST, 0)

    def block_at(i, size):
        return (i * size // low, 0, lax.rem(i, low // size), 0, 0)

    weight_spec = pl.BlockSpec((1, taken * width, hidden_units), lambda i: (0, first(i), 0))
    return pl.pallas_call(
        expert_kernel,
        grid=(FIRST + SECOND,),
        in_specs=[
            pl.BlockSpec((1, groups, taken, slots, width), lambda i: block_at(first(i), taken)),
            weight_spec,
            weight_spec,
            pl.BlockSpec((1, hidden_units, given * width), lambda i: (0, 0, second(i))),
        ],
        out_specs=pl.BlockSpec(
            (1, groups, given, slots, width), lambda i: block_at(second(i), given)
        ),
        out_shape=jax.ShapeDtypeStruct(rows.shape, BF16),
        scratch_shapes=[
            pltpu.VMEM((count, hidden_units), F32),
            pltpu.VMEM((count, hidden_units), F32),
            pltpu.VMEM((count, HEAD), F32),
            pltpu.VMEM((count, hidden_units), BF16),
        ],
        compiler_params=pltpu.CompilerParams(vmem_limit_bytes=56 << 20),
        name="expert",
    )(rows, gate_w, up_w, down_w)


def combine_kernel(slots, weights, answers, hidden, out, accum):
    step = pl.program_id(0)
    tokens = hidden.shape[0]
    count = answers.shape[0]

    @pl.when(step == 0)
    def _():
        accum[...] = hidden[...].astype(F32)

    row = lax.broadcasted_iota(jnp.int32, (SLOTS, tokens), 0).astype(F32)
    mine, scale = slots[...], weights[...]
    picks = [
        jnp.where(mine[e : e + 1, :] == row, scale[e : e + 1, :], 0.0).astype(BF16)
        for e in range(count)
    ]
    total = accum[...] + lax.dot_general(
        jnp.concatenate(picks, axis=0),
        answers[...].reshape(count * SLOTS, answers.shape[2]),
        (((0,), (0,)), ((), ())),
        preferred_element_type=F32,
    )
    accum[...] = total

    @pl.when(step == pl.num_programs(0) - 1)
    def _():
        out[...] = total.astype(BF16)


def combine(slots, weights, answers, hidden):
    tokens, width = hidden.shape
    experts = answers.shape[0]
    count = 16
    return pl.pallas_call(
        combine_kernel,
        grid=(experts // count,),
        in_specs=[
            pl.BlockSpec((count, tokens), lambda i: (i, 0)),
            pl.BlockSpec((count, tokens), lambda i: (i, 0)),
            pl.BlockSpec((count, SLOTS, width), lambda i: (i, 0, 0)),
            pl.BlockSpec((tokens, width), lambda i: (0, 0)),
        ],
        out_specs=pl.BlockSpec((tokens, width), lambda i: (0, 0)),
        out_shape=jax.ShapeDtypeStruct((tokens, width), BF16),
        scratch_shapes=[pltpu.VMEM((tokens, width), F32)],
        compiler_params=pltpu.CompilerParams(vmem_limit_bytes=32 << 20),
        name="combine",
    )(slots, weights, answers, hidden)


def gather_row(rotated_keys, value_matrix):
    own = jnp.concatenate([rotated_keys, value_matrix], axis=1)
    row = [own] + [lax.ppermute(own, "x", rotated(4, k)) for k in range(1, 4)]
    return jnp.concatenate(row)


def shift_row(row):
    return [lax.ppermute(row, ("zh", "y"), rotated(8, k)) for k in range(1, 5)]


def gather_kv(row, shifted):
    tokens = row.shape[0] // 4
    x, core = lax.axis_index("x"), lax.axis_index("c")
    slab = lax.axis_index(("zh", "y"))
    middle, oldest = shifted[:3], shifted[3]
    steps = jnp.arange(1, 4, dtype=jnp.int32)
    near = steps <= x
    picked = jnp.where(jnp.repeat(near, tokens)[:, None], row[tokens:], oldest[tokens:])
    mine = jnp.concatenate([row[:tokens], oldest[:tokens], picked] + middle)
    other = lax.ppermute(mine, "c", flipped(2, 1))

    back = jnp.concatenate(
        [jnp.array([0, 4], jnp.int32), jnp.where(near, 0, 4), jnp.repeat(steps, 4)]
    )
    turn = jnp.array([0, 0, 1, 2, 3] + [0, 1, 2, 3] * 3, jnp.int32)
    begin = ((slab - back) % 8) * 8 + ((x - turn) % 4) * 2
    begin = begin[None, :] + (core ^ jnp.arange(2, dtype=jnp.int32))[:, None]
    pos = begin[:, :, None] * tokens + jnp.arange(tokens, dtype=jnp.int32)
    chunks = begin[:, 5:].reshape(6, 4)
    low = jnp.min(chunks, axis=1) * tokens
    high = jnp.max(chunks, axis=1) * tokens + tokens - 1
    return mine, other, pos.reshape(2, 1, 17 * tokens), low, high


def gather_attended(own):
    def both(block):
        return [block, lax.ppermute(block, "c", flipped(2, 1))]

    near = lax.ppermute(own, Z, flipped(4, 1))
    far = lax.ppermute(own, Z, flipped(4, 3))
    cut = own.shape[0] // 2
    first = lax.ppermute(near[:cut], Z, flipped(4, 3))
    second = lax.ppermute(far[cut:], Z, flipped(4, 1))
    return both(own) + both(near) + both(far) + both(first) + both(second)


def body(
    queries,
    rotated_keys,
    value_matrix,
    lengths,
    out_weight,
    residual,
    expert_ids,
    router_gates,
    gate_proj,
    up_proj,
    down_proj,
):
    tokens = queries.shape[0]
    own_rows, model_width = residual.shape
    experts = 2 * 4 * 4 * 2 * 2
    width = model_width // GROUP

    row = gather_row(rotated_keys, value_matrix)

    weight_rows = out_weight.shape[0]
    meta = jnp.concatenate([expert_ids.astype(BF16), router_gates.astype(BF16)], axis=1)
    meta = meta.reshape(-1, width)
    used = meta.shape[0]
    meta = jnp.pad(meta, ((0, 16 - used), (0, 0)))
    sent = jnp.concatenate(
        [
            out_weight.reshape(weight_rows, GROUP, width).transpose(1, 0, 2),
            residual.reshape(own_rows, GROUP, width).transpose(1, 0, 2),
            jnp.broadcast_to(meta[None], (GROUP, 16, width)),
        ],
        axis=1,
    )
    got = lax.all_to_all(sent, LINE, split_axis=0, concat_axis=0, tiled=True)
    got, row = lax.optimization_barrier((got, row))
    shifted = shift_row(row)
    kv, other, key_pos, low, high = gather_kv(row, shifted)
    weight = lax.all_gather(got[:, :weight_rows], ("y", "x"), axis=0, tiled=True)
    weight = weight.reshape(4, 4, GROUP, weight_rows, width)
    line_residual = got[:, weight_rows : weight_rows + own_rows]
    meta = got[:, weight_rows + own_rows : weight_rows + own_rows + used]
    meta = meta.reshape(GROUP * own_rows, 16).T
    ids = meta[:8].astype(jnp.int32)
    gates = meta[8:].astype(F32)
    slots, weights = route(ids, gates, experts)

    query_pos = lax.axis_index(("zh", "y", "x", "c")) * tokens + jnp.arange(tokens, dtype=jnp.int32)
    starts = jnp.cumsum(lengths) - lengths
    query_start = jnp.max(
        jnp.where(starts[None, :] <= query_pos[:, None], starts[None, :], 0), axis=1
    ).astype(jnp.int32)
    lim = jnp.stack([query_pos[0], query_pos[-1], query_start[0], query_start[-1]])
    line_residual, slots, weights, queries = lax.optimization_barrier(
        (line_residual, slots, weights, queries)
    )
    attended = attend(
        queries, kv, other, key_pos, low, high, lim, query_pos[:, None], query_start[:, None]
    )

    zl, core, zh = lax.axis_index("zl"), lax.axis_index("c"), lax.axis_index("zh")
    halves = []
    for high_part in range(2):
        for c in range(2):
            for k in range(2):
                halves.append((high_part * 2 + c) * 2 + (zl ^ k))
    places = [(zh ^ h) * 2 + (core ^ c) for h in range(2) for c in range(2)]
    table = jnp.stack(halves + places).astype(jnp.int32)
    hidden, outgoing = project(table, gather_attended(attended), weight, line_residual, slots)
    incoming = lax.all_to_all(outgoing, AXES, split_axis=0, concat_axis=0, tiled=True)
    produced = expert(
        incoming.reshape(2, 16, 4, SLOTS, width), gate_proj, up_proj, down_proj
    ).reshape(experts, SLOTS, width)
    answers = lax.all_to_all(produced, AXES, split_axis=0, concat_axis=0, tiled=True)
    mixed = combine(slots, weights, answers, hidden)
    final = lax.all_to_all(
        mixed.reshape(GROUP, own_rows, width), LINE, split_axis=0, concat_axis=0, tiled=True
    )
    return final.transpose(1, 0, 2).reshape(own_rows, model_width)


def solution(mesh):
    fine = Mesh(mesh.devices.reshape(2, 4, 4, 2, 2), AXES)
    ctx = ("zh", "y", "x", "c")
    both = P(AXES, None)
    in_specs = (
        P(ctx, "zl"),
        P(ctx, "zl"),
        P(ctx, "zl"),
        P(),
        P(("zl",) + ctx, None),
        both,
        both,
        both,
        P(AXES, None, None),
        P(AXES, None, None),
        P(AXES, None, None),
    )
    return jax.shard_map(body, mesh=fine, in_specs=in_specs, out_specs=both, check_vma=False)
```

```python
import functools
import math

import jax
import jax.numpy as jnp
from jax import lax
from jax.experimental import pallas as pl
from jax.experimental.pallas import tpu as pltpu
from jax.sharding import Mesh
from jax.sharding import PartitionSpec as P

HEAD = 128
CAP = 6
ROWS = 64
GROUP = 8
SLOTS = GROUP * CAP
CHUNK = 512
EDGE = 640
FIRST, SECOND = 4, 2
NEG = -1e30
BF16 = jnp.bfloat16
F32 = jnp.float32
AXES = ("zh", "y", "x", "c", "zl")
LINE = ("zh", "c", "zl")
Z = ("zh", "zl")


def rotated(count, step):
    return [(i, (i + step) % count) for i in range(count)]


def flipped(count, bits):
    return [(i, i ^ bits) for i in range(count)]


def attention_kernel(lim, low, high, q, kv, other, kpos, qpos, qstart, out, best, accum):
    scale = math.log2(math.e) / math.sqrt(HEAD)
    heads = q.shape[1] // HEAD
    tokens = q.shape[0]
    best[...] = jnp.full(best.shape, NEG, F32)
    accum[...] = jnp.zeros(accum.shape, F32)

    def update(source, begin, count, allowed):
        keys = source[pl.ds(begin, count), :HEAD]
        values = source[pl.ds(begin, count), HEAD:]
        values = jnp.concatenate([values, jnp.ones((count, HEAD), BF16)], axis=1)
        for head in range(heads):
            rows = pl.ds(head * tokens, tokens)
            scores = lax.dot_general(
                q[:, head * HEAD : (head + 1) * HEAD],
                keys,
                (((1,), (1,)), ((), ())),
                preferred_element_type=F32,
            )
            if allowed is not None:
                scores = jnp.where(allowed, scores, NEG)
            old = best[rows, :]
            new = jnp.maximum(old, jnp.max(scores, axis=1, keepdims=True))
            factor = jnp.exp2((old - new) * scale)
            expo = jnp.exp2((scores - jnp.concatenate([new] * (count // HEAD), axis=1)) * scale)
            added = jnp.dot(expo.astype(BF16), values, preferred_element_type=F32)
            accum[rows, :] = accum[rows, :] * jnp.concatenate([factor, factor], axis=1) + added
            best[rows, :] = new

    def inside(at):
        return (at <= qpos[...]) & (at >= qstart[...])

    for side, source in enumerate((kv, other)):
        update(source, 0, EDGE, inside(kpos[side, :, :EDGE]))

    full = (kv.shape[0] - EDGE) // CHUNK
    for side, source in enumerate((kv, other)):

        def step(i, carry, side=side, source=source):
            number = side * full + i
            used = (low[number] <= lim[1]) & (high[number] >= lim[2])
            whole = (high[number] <= lim[0]) & (low[number] >= lim[3])
            begin = pl.multiple_of(EDGE + i * CHUNK, HEAD)

            @pl.when(used & whole)
            def _():
                update(source, begin, CHUNK, None)

            @pl.when(used & jnp.logical_not(whole))
            def _():
                at = kpos[side, :, pl.ds(begin, CHUNK)]
                update(source, begin, CHUNK, inside(at))

            return carry

        lax.fori_loop(0, full, step, 0)

    for head in range(heads):
        rows = pl.ds(head * tokens, tokens)
        state = accum[rows, :]
        out[:, head * HEAD : (head + 1) * HEAD] = (state[:, :HEAD] / state[:, HEAD:]).astype(BF16)


def attend(queries, kv, other, key_pos, low, high, lim, query_pos, query_start):
    tokens, width = queries.shape
    smem = pl.BlockSpec(memory_space=pltpu.SMEM)
    vmem = pl.BlockSpec(memory_space=pltpu.VMEM)
    rows = width // HEAD * tokens
    return pl.pallas_call(
        attention_kernel,
        in_specs=[smem] * 3 + [vmem] * 6,
        out_specs=vmem,
        out_shape=jax.ShapeDtypeStruct((tokens, width), BF16),
        scratch_shapes=[pltpu.VMEM((rows, HEAD), F32), pltpu.VMEM((rows, 2 * HEAD), F32)],
        compiler_params=pltpu.CompilerParams(vmem_limit_bytes=32 << 20),
        cost_estimate=pl.CostEstimate(
            flops=10_000_000_000, bytes_accessed=4_000_000, transcendentals=8_000_000
        ),
        name="attention",
    )(lim, low, high, queries, kv, other, key_pos, query_pos, query_start)


def projection_kernel(steps, *refs):
    slot = refs[0]
    weight, residual, slots, hidden, outgoing, accum = refs[21:]
    step = pl.program_id(0)
    blocks, rows_each, width = residual.shape
    tokens = blocks * rows_each
    count = outgoing.shape[0]

    @pl.when(step < steps)
    def _():
        total = None
        for high in range(2):
            own, own_c, near, near_c, far, far_c, first, first_c, second, second_c = refs[
                1 + high : 21 : 2
            ]
            rows = ((own, own_c, first, second, first_c, second_c), (near, near_c, far, far_c))
            for other in range(2):
                pieces = []
                for x in range(4):
                    for core in range(2):
                        pieces.append(weight[0, x, slot[(high * 2 + core) * 2 + other]])
                part = jnp.dot(
                    jnp.concatenate([ref[...] for ref in rows[other]], axis=0),
                    jnp.concatenate(pieces, axis=0),
                    preferred_element_type=F32,
                )
                total = part if total is None else total + part

        @pl.when(step == 0)
        def _():
            accum[...] = total

        @pl.when(step > 0)
        def _():
            accum[...] += total

    @pl.when(step == steps - 1)
    def _():
        share = tokens // 4
        for block in range(4):
            place = slot[8 + block]
            part = accum[block * share : (block + 1) * share, :]
            base = jnp.concatenate([residual[2 * place], residual[2 * place + 1]], axis=0)
            here = pl.ds(pl.multiple_of(place * share, share), share)
            hidden[here, :] = (base.astype(F32) + part).astype(BF16)

    @pl.when(step >= steps)
    def _():
        row = lax.broadcasted_iota(jnp.int32, (SLOTS, tokens), 0).astype(F32)
        mine = slots[...]
        picks = [jnp.where(mine[e : e + 1, :] == row, 1.0, 0.0).astype(BF16) for e in range(count)]
        sent = jnp.dot(jnp.concatenate(picks, axis=0), hidden[...], preferred_element_type=F32)
        outgoing[...] = sent.astype(BF16).reshape(outgoing.shape)


def project(slot, blocks, weight, residual, slots):
    width = residual.shape[2]
    tokens = residual.shape[0] * residual.shape[1]
    experts = slots.shape[0]
    count = 16
    steps = weight.shape[0]
    depth = blocks[0].shape[1] // (2 * steps)

    def early(k):
        return jnp.minimum(k, steps - 1)

    def late(k):
        return jnp.maximum(k - steps, 0)

    specs = []
    for ref in blocks:
        specs.append(pl.BlockSpec((ref.shape[0], depth), lambda k: (0, early(k))))
        specs.append(pl.BlockSpec((ref.shape[0], depth), lambda k: (0, early(k) + steps)))
    return pl.pallas_call(
        functools.partial(projection_kernel, steps),
        grid=(steps + experts // count,),
        in_specs=[pl.BlockSpec(memory_space=pltpu.SMEM)]
        + specs
        + [
            pl.BlockSpec((1,) + weight.shape[1:], lambda k: (early(k), 0, 0, 0, 0)),
            pl.BlockSpec(residual.shape, lambda k: (0, 0, 0)),
            pl.BlockSpec((count, tokens), lambda k: (late(k), 0)),
        ],
        out_specs=(
            pl.BlockSpec((tokens, width), lambda k: (0, 0)),
            pl.BlockSpec((count, SLOTS, width), lambda k: (late(k), 0, 0)),
        ),
        out_shape=(
            jax.ShapeDtypeStruct((tokens, width), BF16),
            jax.ShapeDtypeStruct((experts, SLOTS, width), BF16),
        ),
        scratch_shapes=[pltpu.VMEM((tokens, width), F32)],
        compiler_params=pltpu.CompilerParams(vmem_limit_bytes=36 << 20),
        name="projection",
    )(slot, *[ref for ref in blocks for _ in range(2)], weight, residual, slots)


def slots_of(ids, experts):
    tokens = ids.shape[1]
    expert = lax.broadcasted_iota(jnp.int32, (experts, tokens), 0)
    named = jnp.zeros((experts, tokens), F32)
    for k in range(ids.shape[0]):
        named = named + jnp.where(ids[k : k + 1, :] == expert, 1.0, 0.0)
    first = lax.broadcasted_iota(jnp.int32, (tokens, tokens), 0)
    second = lax.broadcasted_iota(jnp.int32, (tokens, tokens), 1)
    before = (first < second) & (first // ROWS == second // ROWS)
    rank = jnp.dot(
        named.astype(BF16), jnp.where(before, 1.0, 0.0).astype(BF16), preferred_element_type=F32
    )
    block = lax.broadcasted_iota(jnp.int32, (experts, tokens), 1) // ROWS
    return jnp.where(named > 0, rank + (block * CAP).astype(F32), -1.0)


def routing_kernel(ids, gates, slots, weights):
    experts, tokens = slots.shape
    slots[...] = slots_of(ids[...], experts)
    number = lax.broadcasted_iota(jnp.int32, (experts, tokens), 0)
    total = jnp.zeros((experts, tokens), F32)
    for k in range(ids.shape[0]):
        total = total + jnp.where(ids[k : k + 1, :] == number, gates[k : k + 1, :], 0.0)
    weights[...] = total


def route(ids, gates, experts):
    shape = jax.ShapeDtypeStruct((experts, ids.shape[1]), F32)
    return pl.pallas_call(
        routing_kernel,
        out_shape=(shape, shape),
        compiler_params=pltpu.CompilerParams(vmem_limit_bytes=16 << 20),
        name="routing",
    )(ids, gates)


def expert_kernel(rows, gate_w, up_w, down_w, out, gate, up, squares, act):
    step = pl.program_id(0)
    groups, taken, slots, width = rows.shape[1:]
    count = groups * slots
    model_width = gate_w.shape[1] * FIRST

    @pl.when(step < FIRST)
    def _():
        block = jnp.concatenate(
            [rows[0, :, i].reshape(count, width) for i in range(taken)], axis=1
        )
        gate_part = jnp.dot(block, gate_w[0], preferred_element_type=F32)
        up_part = jnp.dot(block, up_w[0], preferred_element_type=F32)
        wide = block.astype(F32)
        wide = wide * wide
        total = wide[:, :HEAD]
        for i in range(1, taken * width // HEAD):
            total = total + wide[:, i * HEAD : (i + 1) * HEAD]

        @pl.when(step == 0)
        def _():
            gate[...] = gate_part
            up[...] = up_part
            squares[...] = total

        @pl.when(step > 0)
        def _():
            gate[...] += gate_part
            up[...] += up_part
            squares[...] += total

    @pl.when(step == FIRST - 1)
    def _():
        mean = jnp.sum(squares[...], axis=1, keepdims=True) / model_width
        factor = lax.rsqrt(mean + 1e-06)
        value = gate[...] * factor
        act[...] = (value / (1.0 + jnp.exp(-value)) * (up[...] * factor)).astype(BF16)

    @pl.when(step >= FIRST)
    def _():
        result = jnp.dot(act[...], down_w[0], preferred_element_type=F32).astype(BF16)
        for i in range(out.shape[2]):
            out[0, :, i] = result[:, i * width : (i + 1) * width].reshape(groups, slots, width)


def expert(rows, gate_w, up_w, down_w):
    high, groups, low, slots, width = rows.shape
    hidden_units = gate_w.shape[2]
    count = groups * slots
    taken, given = high * low // FIRST, high * low // SECOND

    def first(i):
        return jnp.minimum(i, FIRST - 1)

    def second(i):
        return jnp.maximum(i - FIRST, 0)

    def block_at(i, size):
        return (i * size // low, 0, lax.rem(i, low // size), 0, 0)

    weight_spec = pl.BlockSpec((1, taken * width, hidden_units), lambda i: (0, first(i), 0))
    return pl.pallas_call(
        expert_kernel,
        grid=(FIRST + SECOND,),
        in_specs=[
            pl.BlockSpec((1, groups, taken, slots, width), lambda i: block_at(first(i), taken)),
            weight_spec,
            weight_spec,
            pl.BlockSpec((1, hidden_units, given * width), lambda i: (0, 0, second(i))),
        ],
        out_specs=pl.BlockSpec(
            (1, groups, given, slots, width), lambda i: block_at(second(i), given)
        ),
        out_shape=jax.ShapeDtypeStruct(rows.shape, BF16),
        scratch_shapes=[
            pltpu.VMEM((count, hidden_units), F32),
            pltpu.VMEM((count, hidden_units), F32),
            pltpu.VMEM((count, HEAD), F32),
            pltpu.VMEM((count, hidden_units), BF16),
        ],
        compiler_params=pltpu.CompilerParams(vmem_limit_bytes=56 << 20),
        name="expert",
    )(rows, gate_w, up_w, down_w)


def combine_kernel(slots, weights, answers, hidden, out, accum):
    step = pl.program_id(0)
    tokens = hidden.shape[0]
    count = answers.shape[0]

    @pl.when(step == 0)
    def _():
        accum[...] = hidden[...].astype(F32)

    row = lax.broadcasted_iota(jnp.int32, (SLOTS, tokens), 0).astype(F32)
    mine, scale = slots[...], weights[...]
    picks = [
        jnp.where(mine[e : e + 1, :] == row, scale[e : e + 1, :], 0.0).astype(BF16)
        for e in range(count)
    ]
    total = accum[...] + lax.dot_general(
        jnp.concatenate(picks, axis=0),
        answers[...].reshape(count * SLOTS, answers.shape[2]),
        (((0,), (0,)), ((), ())),
        preferred_element_type=F32,
    )
    accum[...] = total

    @pl.when(step == pl.num_programs(0) - 1)
    def _():
        out[...] = total.astype(BF16)


def combine(slots, weights, answers, hidden):
    tokens, width = hidden.shape
    experts = answers.shape[0]
    count = 16
    return pl.pallas_call(
        combine_kernel,
        grid=(experts // count,),
        in_specs=[
            pl.BlockSpec((count, tokens), lambda i: (i, 0)),
            pl.BlockSpec((count, tokens), lambda i: (i, 0)),
            pl.BlockSpec((count, SLOTS, width), lambda i: (i, 0, 0)),
            pl.BlockSpec((tokens, width), lambda i: (0, 0)),
        ],
        out_specs=pl.BlockSpec((tokens, width), lambda i: (0, 0)),
        out_shape=jax.ShapeDtypeStruct((tokens, width), BF16),
        scratch_shapes=[pltpu.VMEM((tokens, width), F32)],
        compiler_params=pltpu.CompilerParams(vmem_limit_bytes=32 << 20),
        name="combine",
    )(slots, weights, answers, hidden)


def gather_row(rotated_keys, value_matrix):
    own = jnp.concatenate([rotated_keys, value_matrix], axis=1)
    row = [own] + [lax.ppermute(own, "x", rotated(4, k)) for k in range(1, 4)]
    return jnp.concatenate(row)


def shift_row(row, step):
    return lax.ppermute(row, ("zh", "y"), rotated(8, step))


def gather_kv(row, shifted):
    tokens = row.shape[0] // 4
    x, core = lax.axis_index("x"), lax.axis_index("c")
    slab = lax.axis_index(("zh", "y"))
    middle, oldest = shifted[:3], shifted[3]
    steps = jnp.arange(1, 4, dtype=jnp.int32)
    near = steps <= x
    picked = jnp.where(jnp.repeat(near, tokens)[:, None], row[tokens:], oldest[tokens:])
    mine = jnp.concatenate([row[:tokens], oldest[:tokens], picked] + middle)
    other = lax.ppermute(mine, "c", flipped(2, 1))

    back = jnp.concatenate(
        [jnp.array([0, 4], jnp.int32), jnp.where(near, 0, 4), jnp.repeat(steps, 4)]
    )
    turn = jnp.array([0, 0, 1, 2, 3] + [0, 1, 2, 3] * 3, jnp.int32)
    begin = ((slab - back) % 8) * 8 + ((x - turn) % 4) * 2
    begin = begin[None, :] + (core ^ jnp.arange(2, dtype=jnp.int32))[:, None]
    pos = begin[:, :, None] * tokens + jnp.arange(tokens, dtype=jnp.int32)
    chunks = begin[:, 5:].reshape(6, 4)
    low = jnp.min(chunks, axis=1) * tokens
    high = jnp.max(chunks, axis=1) * tokens + tokens - 1
    return mine, other, pos.reshape(2, 1, 17 * tokens), low, high


def gather_attended(own, others):
    def both(block):
        return [block, lax.ppermute(block, "c", flipped(2, 1))]

    near = lax.ppermute(own, Z, flipped(4, 1))
    far = lax.ppermute(own, Z, flipped(4, 3))
    near, far, *others = lax.optimization_barrier((near, far, *others))
    cut = own.shape[0] // 2
    first = lax.ppermute(near[:cut], Z, flipped(4, 3))
    second = lax.ppermute(far[cut:], Z, flipped(4, 1))
    return both(own) + both(near) + both(far) + both(first) + both(second), others


def body(
    queries,
    rotated_keys,
    value_matrix,
    lengths,
    out_weight,
    residual,
    expert_ids,
    router_gates,
    gate_proj,
    up_proj,
    down_proj,
):
    tokens = queries.shape[0]
    own_rows, model_width = residual.shape
    experts = 2 * 4 * 4 * 2 * 2
    width = model_width // GROUP

    row = gather_row(rotated_keys, value_matrix)

    weight_rows = out_weight.shape[0]
    meta = jnp.concatenate([expert_ids.astype(BF16), router_gates.astype(BF16)], axis=1)
    meta = meta.reshape(-1, width)
    used = meta.shape[0]
    meta = jnp.pad(meta, ((0, 16 - used), (0, 0)))
    sent = jnp.concatenate(
        [
            out_weight.reshape(weight_rows, GROUP, width).transpose(1, 0, 2),
            residual.reshape(own_rows, GROUP, width).transpose(1, 0, 2),
            jnp.broadcast_to(meta[None], (GROUP, 16, width)),
        ],
        axis=1,
    )
    before, third = shift_row(row, 1), shift_row(row, 3)
    sent, before, third = lax.optimization_barrier((sent, before, third))
    got = lax.all_to_all(sent, LINE, split_axis=0, concat_axis=0, tiled=True)
    half = row.shape[0] // 2
    got, second, rest, oldest = lax.optimization_barrier(
        (got, shift_row(before[:half], 1), shift_row(third[half:], -1), shift_row(row, 4))
    )
    shifted = [before, jnp.concatenate([second, rest]), third, oldest]
    kv, other, key_pos, low, high = gather_kv(row, shifted)
    weight = lax.all_gather(got[:, :weight_rows], ("y", "x"), axis=0, tiled=True)
    weight = weight.reshape(4, 4, GROUP, weight_rows, width)
    line_residual = got[:, weight_rows : weight_rows + own_rows]
    meta = got[:, weight_rows + own_rows : weight_rows + own_rows + used]
    meta = meta.reshape(GROUP * own_rows, 16).T
    ids = meta[:8].astype(jnp.int32)
    gates = meta[8:].astype(F32)
    slots, weights = route(ids, gates, experts)

    query_pos = lax.axis_index(("zh", "y", "x", "c")) * tokens + jnp.arange(tokens, dtype=jnp.int32)
    starts = jnp.cumsum(lengths) - lengths
    query_start = jnp.max(
        jnp.where(starts[None, :] <= query_pos[:, None], starts[None, :], 0), axis=1
    ).astype(jnp.int32)
    lim = jnp.stack([query_pos[0], query_pos[-1], query_start[0], query_start[-1]])
    attended = attend(
        queries, kv, other, key_pos, low, high, lim, query_pos[:, None], query_start[:, None]
    )

    zl, core, zh = lax.axis_index("zl"), lax.axis_index("c"), lax.axis_index("zh")
    halves = []
    for high_part in range(2):
        for c in range(2):
            for k in range(2):
                halves.append((high_part * 2 + c) * 2 + (zl ^ k))
    places = [(zh ^ h) * 2 + (core ^ c) for h in range(2) for c in range(2)]
    table = jnp.stack(halves + places).astype(jnp.int32)
    blocks, (line_residual, slots, weights) = gather_attended(
        attended, (line_residual, slots, weights)
    )
    hidden, outgoing = project(table, blocks, weight, line_residual, slots)
    incoming = lax.all_to_all(outgoing, AXES, split_axis=0, concat_axis=0, tiled=True)
    produced = expert(
        incoming.reshape(2, 16, 4, SLOTS, width), gate_proj, up_proj, down_proj
    ).reshape(experts, SLOTS, width)
    answers = lax.all_to_all(produced, AXES, split_axis=0, concat_axis=0, tiled=True)
    mixed = combine(slots, weights, answers, hidden)
    final = lax.all_to_all(
        mixed.reshape(GROUP, own_rows, width), LINE, split_axis=0, concat_axis=0, tiled=True
    )
    return final.transpose(1, 0, 2).reshape(own_rows, model_width)


def solution(mesh):
    fine = Mesh(mesh.devices.reshape(2, 4, 4, 2, 2), AXES)
    ctx = ("zh", "y", "x", "c")
    both = P(AXES, None)
    in_specs = (
        P(ctx, "zl"),
        P(ctx, "zl"),
        P(ctx, "zl"),
        P(),
        P(("zl",) + ctx, None),
        both,
        both,
        both,
        P(AXES, None, None),
        P(AXES, None, None),
        P(AXES, None, None),
    )
    return jax.shard_map(body, mesh=fine, in_specs=in_specs, out_specs=both, check_vma=False)
```

```python
import functools
import math

import jax
import jax.numpy as jnp
from jax import lax
from jax.experimental import pallas as pl
from jax.experimental.pallas import tpu as pltpu
from jax.sharding import Mesh
from jax.sharding import PartitionSpec as P

HEAD = 128
CAP = 6
ROWS = 64
GROUP = 8
SLOTS = GROUP * CAP
CHUNK = 512
EDGE = 640
FIRST, SECOND = 4, 2
NEG = -1e30
BF16 = jnp.bfloat16
F32 = jnp.float32
AXES = ("zh", "y", "x", "c", "zl")
LINE = ("zh", "c", "zl")
Z = ("zh", "zl")


def rotated(count, step):
    return [(i, (i + step) % count) for i in range(count)]


def flipped(count, bits):
    return [(i, i ^ bits) for i in range(count)]


def attention_kernel(lim, low, high, q, kv, other, kpos, qpos, qstart, out, best, accum):
    scale = math.log2(math.e) / math.sqrt(HEAD)
    heads = q.shape[1] // HEAD
    tokens = q.shape[0]
    best[...] = jnp.full(best.shape, NEG, F32)
    accum[...] = jnp.zeros(accum.shape, F32)

    def update(source, begin, count, allowed):
        keys = source[pl.ds(begin, count), :HEAD]
        values = source[pl.ds(begin, count), HEAD:]
        values = jnp.concatenate([values, jnp.ones((count, HEAD), BF16)], axis=1)
        for head in range(heads):
            rows = pl.ds(head * tokens, tokens)
            scores = lax.dot_general(
                q[:, head * HEAD : (head + 1) * HEAD],
                keys,
                (((1,), (1,)), ((), ())),
                preferred_element_type=F32,
            )
            if allowed is not None:
                scores = jnp.where(allowed, scores, NEG)
            old = best[rows, :]
            new = jnp.maximum(old, jnp.max(scores, axis=1, keepdims=True))
            factor = jnp.exp2((old - new) * scale)
            expo = jnp.exp2((scores - jnp.concatenate([new] * (count // HEAD), axis=1)) * scale)
            added = jnp.dot(expo.astype(BF16), values, preferred_element_type=F32)
            accum[rows, :] = accum[rows, :] * jnp.concatenate([factor, factor], axis=1) + added
            best[rows, :] = new

    def inside(at):
        return (at <= qpos[...]) & (at >= qstart[...])

    for side, source in enumerate((kv, other)):
        update(source, 0, EDGE, inside(kpos[side, :, :EDGE]))

    full = (kv.shape[0] - EDGE) // CHUNK
    for side, source in enumerate((kv, other)):

        def step(i, carry, side=side, source=source):
            number = side * full + i
            used = (low[number] <= lim[1]) & (high[number] >= lim[2])
            whole = (high[number] <= lim[0]) & (low[number] >= lim[3])
            begin = pl.multiple_of(EDGE + i * CHUNK, HEAD)

            @pl.when(used & whole)
            def _():
                update(source, begin, CHUNK, None)

            @pl.when(used & jnp.logical_not(whole))
            def _():
                at = kpos[side, :, pl.ds(begin, CHUNK)]
                update(source, begin, CHUNK, inside(at))

            return carry

        lax.fori_loop(0, full, step, 0)

    for head in range(heads):
        rows = pl.ds(head * tokens, tokens)
        state = accum[rows, :]
        out[:, head * HEAD : (head + 1) * HEAD] = (state[:, :HEAD] / state[:, HEAD:]).astype(BF16)


def attend(queries, kv, other, key_pos, low, high, lim, query_pos, query_start):
    tokens, width = queries.shape
    smem = pl.BlockSpec(memory_space=pltpu.SMEM)
    vmem = pl.BlockSpec(memory_space=pltpu.VMEM)
    rows = width // HEAD * tokens
    return pl.pallas_call(
        attention_kernel,
        in_specs=[smem] * 3 + [vmem] * 6,
        out_specs=vmem,
        out_shape=jax.ShapeDtypeStruct((tokens, width), BF16),
        scratch_shapes=[pltpu.VMEM((rows, HEAD), F32), pltpu.VMEM((rows, 2 * HEAD), F32)],
        compiler_params=pltpu.CompilerParams(vmem_limit_bytes=32 << 20),
        cost_estimate=pl.CostEstimate(
            flops=10_000_000_000, bytes_accessed=4_000_000, transcendentals=8_000_000
        ),
        name="attention",
    )(lim, low, high, queries, kv, other, key_pos, query_pos, query_start)


def projection_kernel(steps, *refs):
    slot = refs[0]
    weight, residual, slots, hidden, outgoing, accum = refs[21:]
    step = pl.program_id(0)
    blocks, rows_each, width = residual.shape
    tokens = blocks * rows_each
    count = outgoing.shape[0]

    @pl.when(step < steps)
    def _():
        total = None
        for high in range(2):
            own, own_c, near, near_c, far, far_c, first, first_c, second, second_c = refs[
                1 + high : 21 : 2
            ]
            rows = ((own, own_c, first, second, first_c, second_c), (near, near_c, far, far_c))
            for other in range(2):
                pieces = []
                for x in range(4):
                    for core in range(2):
                        pieces.append(weight[0, x, slot[(high * 2 + core) * 2 + other]])
                part = jnp.dot(
                    jnp.concatenate([ref[...] for ref in rows[other]], axis=0),
                    jnp.concatenate(pieces, axis=0),
                    preferred_element_type=F32,
                )
                total = part if total is None else total + part

        @pl.when(step == 0)
        def _():
            accum[...] = total

        @pl.when(step > 0)
        def _():
            accum[...] += total

    @pl.when(step == steps - 1)
    def _():
        share = tokens // 4
        for block in range(4):
            place = slot[8 + block]
            part = accum[block * share : (block + 1) * share, :]
            base = jnp.concatenate([residual[2 * place], residual[2 * place + 1]], axis=0)
            here = pl.ds(pl.multiple_of(place * share, share), share)
            hidden[here, :] = (base.astype(F32) + part).astype(BF16)

    @pl.when(step >= steps)
    def _():
        row = lax.broadcasted_iota(jnp.int32, (SLOTS, tokens), 0).astype(F32)
        mine = slots[...]
        picks = [jnp.where(mine[e : e + 1, :] == row, 1.0, 0.0).astype(BF16) for e in range(count)]
        sent = jnp.dot(jnp.concatenate(picks, axis=0), hidden[...], preferred_element_type=F32)
        outgoing[...] = sent.astype(BF16).reshape(outgoing.shape)


def project(slot, blocks, weight, residual, slots):
    width = residual.shape[2]
    tokens = residual.shape[0] * residual.shape[1]
    experts = slots.shape[0]
    count = 16
    steps = weight.shape[0]
    depth = blocks[0].shape[1] // (2 * steps)

    def early(k):
        return jnp.minimum(k, steps - 1)

    def late(k):
        return jnp.maximum(k - steps, 0)

    specs = []
    for ref in blocks:
        specs.append(pl.BlockSpec((ref.shape[0], depth), lambda k: (0, early(k))))
        specs.append(pl.BlockSpec((ref.shape[0], depth), lambda k: (0, early(k) + steps)))
    return pl.pallas_call(
        functools.partial(projection_kernel, steps),
        grid=(steps + experts // count,),
        in_specs=[pl.BlockSpec(memory_space=pltpu.SMEM)]
        + specs
        + [
            pl.BlockSpec((1,) + weight.shape[1:], lambda k: (early(k), 0, 0, 0, 0)),
            pl.BlockSpec(residual.shape, lambda k: (0, 0, 0)),
            pl.BlockSpec((count, tokens), lambda k: (late(k), 0)),
        ],
        out_specs=(
            pl.BlockSpec((tokens, width), lambda k: (0, 0)),
            pl.BlockSpec((count, SLOTS, width), lambda k: (late(k), 0, 0)),
        ),
        out_shape=(
            jax.ShapeDtypeStruct((tokens, width), BF16),
            jax.ShapeDtypeStruct((experts, SLOTS, width), BF16),
        ),
        scratch_shapes=[pltpu.VMEM((tokens, width), F32)],
        compiler_params=pltpu.CompilerParams(vmem_limit_bytes=36 << 20),
        name="projection",
    )(slot, *[ref for ref in blocks for _ in range(2)], weight, residual, slots)


def slots_of(ids, experts):
    tokens = ids.shape[1]
    expert = lax.broadcasted_iota(jnp.int32, (experts, tokens), 0)
    named = jnp.zeros((experts, tokens), F32)
    for k in range(ids.shape[0]):
        named = named + jnp.where(ids[k : k + 1, :] == expert, 1.0, 0.0)
    first = lax.broadcasted_iota(jnp.int32, (tokens, tokens), 0)
    second = lax.broadcasted_iota(jnp.int32, (tokens, tokens), 1)
    before = (first < second) & (first // ROWS == second // ROWS)
    rank = jnp.dot(
        named.astype(BF16), jnp.where(before, 1.0, 0.0).astype(BF16), preferred_element_type=F32
    )
    block = lax.broadcasted_iota(jnp.int32, (experts, tokens), 1) // ROWS
    return jnp.where(named > 0, rank + (block * CAP).astype(F32), -1.0)


def routing_kernel(ids, gates, slots, weights):
    experts, tokens = slots.shape
    slots[...] = slots_of(ids[...], experts)
    number = lax.broadcasted_iota(jnp.int32, (experts, tokens), 0)
    total = jnp.zeros((experts, tokens), F32)
    for k in range(ids.shape[0]):
        total = total + jnp.where(ids[k : k + 1, :] == number, gates[k : k + 1, :], 0.0)
    weights[...] = total


def route(ids, gates, experts):
    shape = jax.ShapeDtypeStruct((experts, ids.shape[1]), F32)
    return pl.pallas_call(
        routing_kernel,
        out_shape=(shape, shape),
        compiler_params=pltpu.CompilerParams(vmem_limit_bytes=16 << 20),
        name="routing",
    )(ids, gates)


def expert_kernel(rows, gate_w, up_w, down_w, out, gate, up, squares, act):
    step = pl.program_id(0)
    groups, taken, slots, width = rows.shape[1:]
    count = groups * slots
    model_width = gate_w.shape[1] * FIRST

    @pl.when(step < FIRST)
    def _():
        block = jnp.concatenate(
            [rows[0, :, i].reshape(count, width) for i in range(taken)], axis=1
        )
        gate_part = jnp.dot(block, gate_w[0], preferred_element_type=F32)
        up_part = jnp.dot(block, up_w[0], preferred_element_type=F32)
        wide = block.astype(F32)
        wide = wide * wide
        total = wide[:, :HEAD]
        for i in range(1, taken * width // HEAD):
            total = total + wide[:, i * HEAD : (i + 1) * HEAD]

        @pl.when(step == 0)
        def _():
            gate[...] = gate_part
            up[...] = up_part
            squares[...] = total

        @pl.when(step > 0)
        def _():
            gate[...] += gate_part
            up[...] += up_part
            squares[...] += total

    @pl.when(step == FIRST - 1)
    def _():
        mean = jnp.sum(squares[...], axis=1, keepdims=True) / model_width
        factor = lax.rsqrt(mean + 1e-06)
        value = gate[...] * factor
        act[...] = (value / (1.0 + jnp.exp(-value)) * (up[...] * factor)).astype(BF16)

    @pl.when(step >= FIRST)
    def _():
        result = jnp.dot(act[...], down_w[0], preferred_element_type=F32).astype(BF16)
        for i in range(out.shape[2]):
            out[0, :, i] = result[:, i * width : (i + 1) * width].reshape(groups, slots, width)


def expert(rows, gate_w, up_w, down_w):
    high, groups, low, slots, width = rows.shape
    hidden_units = gate_w.shape[2]
    count = groups * slots
    taken, given = high * low // FIRST, high * low // SECOND

    def first(i):
        return jnp.minimum(i, FIRST - 1)

    def second(i):
        return jnp.maximum(i - FIRST, 0)

    def block_at(i, size):
        return (i * size // low, 0, lax.rem(i, low // size), 0, 0)

    weight_spec = pl.BlockSpec((1, taken * width, hidden_units), lambda i: (0, first(i), 0))
    return pl.pallas_call(
        expert_kernel,
        grid=(FIRST + SECOND,),
        in_specs=[
            pl.BlockSpec((1, groups, taken, slots, width), lambda i: block_at(first(i), taken)),
            weight_spec,
            weight_spec,
            pl.BlockSpec((1, hidden_units, given * width), lambda i: (0, 0, second(i))),
        ],
        out_specs=pl.BlockSpec(
            (1, groups, given, slots, width), lambda i: block_at(second(i), given)
        ),
        out_shape=jax.ShapeDtypeStruct(rows.shape, BF16),
        scratch_shapes=[
            pltpu.VMEM((count, hidden_units), F32),
            pltpu.VMEM((count, hidden_units), F32),
            pltpu.VMEM((count, HEAD), F32),
            pltpu.VMEM((count, hidden_units), BF16),
        ],
        compiler_params=pltpu.CompilerParams(vmem_limit_bytes=56 << 20),
        name="expert",
    )(rows, gate_w, up_w, down_w)


def combine_kernel(slots, weights, answers, hidden, out, accum):
    step = pl.program_id(0)
    tokens = hidden.shape[0]
    count = answers.shape[0]

    @pl.when(step == 0)
    def _():
        accum[...] = hidden[...].astype(F32)

    row = lax.broadcasted_iota(jnp.int32, (SLOTS, tokens), 0).astype(F32)
    mine, scale = slots[...], weights[...]
    picks = [
        jnp.where(mine[e : e + 1, :] == row, scale[e : e + 1, :], 0.0).astype(BF16)
        for e in range(count)
    ]
    total = accum[...] + lax.dot_general(
        jnp.concatenate(picks, axis=0),
        answers[...].reshape(count * SLOTS, answers.shape[2]),
        (((0,), (0,)), ((), ())),
        preferred_element_type=F32,
    )
    accum[...] = total

    @pl.when(step == pl.num_programs(0) - 1)
    def _():
        out[...] = total.astype(BF16)


def combine(slots, weights, answers, hidden):
    tokens, width = hidden.shape
    experts = answers.shape[0]
    count = 32
    return pl.pallas_call(
        combine_kernel,
        grid=(experts // count,),
        in_specs=[
            pl.BlockSpec((count, tokens), lambda i: (i, 0)),
            pl.BlockSpec((count, tokens), lambda i: (i, 0)),
            pl.BlockSpec((count, SLOTS, width), lambda i: (i, 0, 0)),
            pl.BlockSpec((tokens, width), lambda i: (0, 0)),
        ],
        out_specs=pl.BlockSpec((tokens, width), lambda i: (0, 0)),
        out_shape=jax.ShapeDtypeStruct((tokens, width), BF16),
        scratch_shapes=[pltpu.VMEM((tokens, width), F32)],
        compiler_params=pltpu.CompilerParams(vmem_limit_bytes=32 << 20),
        name="combine",
    )(slots, weights, answers, hidden)


def gather_row(rotated_keys, value_matrix):
    own = jnp.concatenate([rotated_keys, value_matrix], axis=1)
    row = [own] + [lax.ppermute(own, "x", rotated(4, k)) for k in range(1, 4)]
    return jnp.concatenate(row)


def shift_row(row, step):
    return lax.ppermute(row, ("zh", "y"), rotated(8, step))


def gather_kv(row, shifted):
    tokens = row.shape[0] // 4
    middle, oldest = shifted[:3], shifted[3]
    near = jnp.arange(1, 4, dtype=jnp.int32) <= lax.axis_index("x")
    picked = jnp.where(jnp.repeat(near, tokens)[:, None], row[tokens:], oldest[tokens:])
    mine = jnp.concatenate([row[:tokens], oldest[:tokens], picked] + middle)
    return mine, lax.ppermute(mine, "c", flipped(2, 1))


def key_tables(tokens):
    x, core = lax.axis_index("x"), lax.axis_index("c")
    slab = lax.axis_index(("zh", "y"))
    steps = jnp.arange(1, 4, dtype=jnp.int32)
    back = jnp.concatenate(
        [jnp.array([0, 4], jnp.int32), jnp.where(steps <= x, 0, 4), jnp.repeat(steps, 4)]
    )
    turn = jnp.array([0, 0, 1, 2, 3] + [0, 1, 2, 3] * 3, jnp.int32)
    begin = ((slab - back) % 8) * 8 + ((x - turn) % 4) * 2
    begin = begin[None, :] + (core ^ jnp.arange(2, dtype=jnp.int32))[:, None]
    pos = begin[:, :, None] * tokens + jnp.arange(tokens, dtype=jnp.int32)
    chunks = begin[:, 5:].reshape(6, 4)
    low = jnp.min(chunks, axis=1) * tokens
    high = jnp.max(chunks, axis=1) * tokens + tokens - 1
    return pos.reshape(2, 1, 17 * tokens), low, high


def query_tables(tokens, lengths):
    query_pos = lax.axis_index(("zh", "y", "x", "c")) * tokens + jnp.arange(tokens, dtype=jnp.int32)
    starts = jnp.cumsum(lengths) - lengths
    query_start = jnp.max(
        jnp.where(starts[None, :] <= query_pos[:, None], starts[None, :], 0), axis=1
    ).astype(jnp.int32)
    lim = jnp.stack([query_pos[0], query_pos[-1], query_start[0], query_start[-1]])
    return lim, query_pos[:, None], query_start[:, None]


def gather_attended(own, others):
    def both(block):
        return [block, lax.ppermute(block, "c", flipped(2, 1))]

    near = lax.ppermute(own, Z, flipped(4, 1))
    far = lax.ppermute(own, Z, flipped(4, 3))
    near, far, *others = lax.optimization_barrier((near, far, *others))
    cut = own.shape[0] // 2
    first = lax.ppermute(near[:cut], Z, flipped(4, 3))
    second = lax.ppermute(far[cut:], Z, flipped(4, 1))
    return both(own) + both(near) + both(far) + both(first) + both(second), others


def body(
    queries,
    rotated_keys,
    value_matrix,
    lengths,
    out_weight,
    residual,
    expert_ids,
    router_gates,
    gate_proj,
    up_proj,
    down_proj,
):
    tokens = queries.shape[0]
    own_rows, model_width = residual.shape
    experts = 2 * 4 * 4 * 2 * 2
    width = model_width // GROUP

    row = gather_row(rotated_keys, value_matrix)

    weight_rows = out_weight.shape[0]
    meta = jnp.concatenate([expert_ids.astype(BF16), router_gates.astype(BF16)], axis=1)
    meta = meta.reshape(-1, width)
    used = meta.shape[0]
    meta = jnp.pad(meta, ((0, 16 - used), (0, 0)))
    sent = jnp.concatenate(
        [
            out_weight.reshape(weight_rows, GROUP, width).transpose(1, 0, 2),
            residual.reshape(own_rows, GROUP, width).transpose(1, 0, 2),
            jnp.broadcast_to(meta[None], (GROUP, 16, width)),
        ],
        axis=1,
    )
    got = lax.all_to_all(sent, LINE, split_axis=0, concat_axis=0, tiled=True)
    tables = key_tables(tokens) + query_tables(tokens, lengths)
    got, before, third, *tables = lax.optimization_barrier(
        (got, shift_row(row, 1), shift_row(row, 3)) + tables
    )
    half = row.shape[0] // 2
    second, rest, oldest = lax.optimization_barrier(
        (shift_row(before[:half], 1), shift_row(third[half:], -1), shift_row(row, 4))
    )
    kv, other = gather_kv(row, [before, jnp.concatenate([second, rest]), third, oldest])
    weight = lax.all_gather(got[:, :weight_rows], ("y", "x"), axis=0, tiled=True)
    weight = weight.reshape(4, 4, GROUP, weight_rows, width)
    line_residual = got[:, weight_rows : weight_rows + own_rows]
    meta = got[:, weight_rows + own_rows : weight_rows + own_rows + used]
    meta = meta.reshape(GROUP * own_rows, 16).T
    ids = meta[:8].astype(jnp.int32)
    gates = meta[8:].astype(F32)
    slots, weights = route(ids, gates, experts)

    attended = attend(queries, kv, other, *tables)

    zl, core, zh = lax.axis_index("zl"), lax.axis_index("c"), lax.axis_index("zh")
    halves = []
    for high_part in range(2):
        for c in range(2):
            for k in range(2):
                halves.append((high_part * 2 + c) * 2 + (zl ^ k))
    places = [(zh ^ h) * 2 + (core ^ c) for h in range(2) for c in range(2)]
    table = jnp.stack(halves + places).astype(jnp.int32)
    blocks, (line_residual, slots, weights, weight) = gather_attended(
        attended, (line_residual, slots, weights, weight)
    )
    hidden, outgoing = project(table, blocks, weight, line_residual, slots)
    incoming = lax.all_to_all(outgoing, AXES, split_axis=0, concat_axis=0, tiled=True)
    produced = expert(
        incoming.reshape(2, 16, 4, SLOTS, width), gate_proj, up_proj, down_proj
    ).reshape(experts, SLOTS, width)
    answers = lax.all_to_all(produced, AXES, split_axis=0, concat_axis=0, tiled=True)
    mixed = combine(slots, weights, answers, hidden)
    final = lax.all_to_all(
        mixed.reshape(GROUP, own_rows, width), LINE, split_axis=0, concat_axis=0, tiled=True
    )
    return final.transpose(1, 0, 2).reshape(own_rows, model_width)


def solution(mesh):
    fine = Mesh(mesh.devices.reshape(2, 4, 4, 2, 2), AXES)
    ctx = ("zh", "y", "x", "c")
    both = P(AXES, None)
    in_specs = (
        P(ctx, "zl"),
        P(ctx, "zl"),
        P(ctx, "zl"),
        P(),
        P(("zl",) + ctx, None),
        both,
        both,
        both,
        P(AXES, None, None),
        P(AXES, None, None),
        P(AXES, None, None),
    )
    return jax.shard_map(body, mesh=fine, in_specs=in_specs, out_specs=both, check_vma=False)
```

```python
import functools
import math

import jax
import jax.numpy as jnp
from jax import lax
from jax.experimental import pallas as pl
from jax.experimental.pallas import tpu as pltpu
from jax.sharding import Mesh
from jax.sharding import PartitionSpec as P

HEAD = 128
CAP = 6
ROWS = 64
GROUP = 8
SLOTS = GROUP * CAP
CHUNK = 512
EDGE = 640
FIRST, SECOND = 4, 2
NEG = -1e30
BF16 = jnp.bfloat16
F32 = jnp.float32
AXES = ("zh", "y", "x", "c", "zl")
LINE = ("zh", "c", "zl")
Z = ("zh", "zl")


def rotated(count, step):
    return [(i, (i + step) % count) for i in range(count)]


def flipped(count, bits):
    return [(i, i ^ bits) for i in range(count)]


def attention_kernel(lim, low, high, q, kv, other, kpos, qpos, qstart, out, best, accum):
    scale = math.log2(math.e) / math.sqrt(HEAD)
    heads = q.shape[1] // HEAD
    tokens = q.shape[0]
    best[...] = jnp.full(best.shape, NEG, F32)
    accum[...] = jnp.zeros(accum.shape, F32)

    def update(source, begin, count, allowed):
        keys = source[pl.ds(begin, count), :HEAD]
        values = source[pl.ds(begin, count), HEAD:]
        values = jnp.concatenate([values, jnp.ones((count, HEAD), BF16)], axis=1)
        for head in range(heads):
            rows = pl.ds(head * tokens, tokens)
            scores = lax.dot_general(
                q[:, head * HEAD : (head + 1) * HEAD],
                keys,
                (((1,), (1,)), ((), ())),
                preferred_element_type=F32,
            )
            if allowed is not None:
                scores = jnp.where(allowed, scores, NEG)
            old = best[rows, :]
            new = jnp.maximum(old, jnp.max(scores, axis=1, keepdims=True))
            factor = jnp.exp2((old - new) * scale)
            expo = jnp.exp2((scores - jnp.concatenate([new] * (count // HEAD), axis=1)) * scale)
            added = jnp.dot(expo.astype(BF16), values, preferred_element_type=F32)
            accum[rows, :] = accum[rows, :] * jnp.concatenate([factor, factor], axis=1) + added
            best[rows, :] = new

    def inside(at):
        return (at <= qpos[...]) & (at >= qstart[...])

    for side, source in enumerate((kv, other)):
        update(source, 0, EDGE, inside(kpos[side, :, :EDGE]))

    full = (kv.shape[0] - EDGE) // CHUNK
    for side, source in enumerate((kv, other)):

        def step(i, carry, side=side, source=source):
            number = side * full + i
            used = (low[number] <= lim[1]) & (high[number] >= lim[2])
            whole = (high[number] <= lim[0]) & (low[number] >= lim[3])
            begin = pl.multiple_of(EDGE + i * CHUNK, HEAD)

            @pl.when(used & whole)
            def _():
                update(source, begin, CHUNK, None)

            @pl.when(used & jnp.logical_not(whole))
            def _():
                at = kpos[side, :, pl.ds(begin, CHUNK)]
                update(source, begin, CHUNK, inside(at))

            return carry

        lax.fori_loop(0, full, step, 0)

    for head in range(heads):
        rows = pl.ds(head * tokens, tokens)
        state = accum[rows, :]
        out[:, head * HEAD : (head + 1) * HEAD] = (state[:, :HEAD] / state[:, HEAD:]).astype(BF16)


def attend(queries, kv, other, key_pos, low, high, lim, query_pos, query_start):
    tokens, width = queries.shape
    smem = pl.BlockSpec(memory_space=pltpu.SMEM)
    vmem = pl.BlockSpec(memory_space=pltpu.VMEM)
    rows = width // HEAD * tokens
    return pl.pallas_call(
        attention_kernel,
        in_specs=[smem] * 3 + [vmem] * 6,
        out_specs=vmem,
        out_shape=jax.ShapeDtypeStruct((tokens, width), BF16),
        scratch_shapes=[pltpu.VMEM((rows, HEAD), F32), pltpu.VMEM((rows, 2 * HEAD), F32)],
        compiler_params=pltpu.CompilerParams(vmem_limit_bytes=32 << 20),
        cost_estimate=pl.CostEstimate(
            flops=10_000_000_000, bytes_accessed=4_000_000, transcendentals=8_000_000
        ),
        name="attention",
    )(lim, low, high, queries, kv, other, key_pos, query_pos, query_start)


def projection_kernel(steps, *refs):
    slot = refs[0]
    weight, residual, slots, hidden, outgoing, accum = refs[21:]
    step = pl.program_id(0)
    blocks, rows_each, width = residual.shape
    tokens = blocks * rows_each
    count = outgoing.shape[0]

    @pl.when(step < steps)
    def _():
        total = None
        for high in range(2):
            own, own_c, near, near_c, far, far_c, first, first_c, second, second_c = refs[
                1 + high : 21 : 2
            ]
            rows = ((own, own_c, first, second, first_c, second_c), (near, near_c, far, far_c))
            for other in range(2):
                pieces = []
                for x in range(4):
                    for core in range(2):
                        pieces.append(weight[0, x, slot[(high * 2 + core) * 2 + other]])
                part = jnp.dot(
                    jnp.concatenate([ref[...] for ref in rows[other]], axis=0),
                    jnp.concatenate(pieces, axis=0),
                    preferred_element_type=F32,
                )
                total = part if total is None else total + part

        @pl.when(step == 0)
        def _():
            accum[...] = total

        @pl.when(step > 0)
        def _():
            accum[...] += total

    @pl.when(step == steps - 1)
    def _():
        share = tokens // 4
        for block in range(4):
            place = slot[8 + block]
            part = accum[block * share : (block + 1) * share, :]
            base = jnp.concatenate([residual[2 * place], residual[2 * place + 1]], axis=0)
            here = pl.ds(pl.multiple_of(place * share, share), share)
            hidden[here, :] = (base.astype(F32) + part).astype(BF16)

    @pl.when(step >= steps)
    def _():
        row = lax.broadcasted_iota(jnp.int32, (SLOTS, tokens), 0).astype(F32)
        mine = slots[...]
        picks = [jnp.where(mine[e : e + 1, :] == row, 1.0, 0.0).astype(BF16) for e in range(count)]
        sent = jnp.dot(jnp.concatenate(picks, axis=0), hidden[...], preferred_element_type=F32)
        outgoing[...] = sent.astype(BF16).reshape(outgoing.shape)


def project(slot, blocks, weight, residual, slots):
    width = residual.shape[2]
    tokens = residual.shape[0] * residual.shape[1]
    experts = slots.shape[0]
    count = 16
    steps = weight.shape[0]
    depth = blocks[0].shape[1] // (2 * steps)

    def early(k):
        return jnp.minimum(k, steps - 1)

    def late(k):
        return jnp.maximum(k - steps, 0)

    specs = []
    for ref in blocks:
        specs.append(pl.BlockSpec((ref.shape[0], depth), lambda k: (0, early(k))))
        specs.append(pl.BlockSpec((ref.shape[0], depth), lambda k: (0, early(k) + steps)))
    return pl.pallas_call(
        functools.partial(projection_kernel, steps),
        grid=(steps + experts // count,),
        in_specs=[pl.BlockSpec(memory_space=pltpu.SMEM)]
        + specs
        + [
            pl.BlockSpec((1,) + weight.shape[1:], lambda k: (early(k), 0, 0, 0, 0)),
            pl.BlockSpec(residual.shape, lambda k: (0, 0, 0)),
            pl.BlockSpec((count, tokens), lambda k: (late(k), 0)),
        ],
        out_specs=(
            pl.BlockSpec((tokens, width), lambda k: (0, 0)),
            pl.BlockSpec((count, SLOTS, width), lambda k: (late(k), 0, 0)),
        ),
        out_shape=(
            jax.ShapeDtypeStruct((tokens, width), BF16),
            jax.ShapeDtypeStruct((experts, SLOTS, width), BF16),
        ),
        scratch_shapes=[pltpu.VMEM((tokens, width), F32)],
        compiler_params=pltpu.CompilerParams(vmem_limit_bytes=36 << 20),
        name="projection",
    )(slot, *[ref for ref in blocks for _ in range(2)], weight, residual, slots)


def slots_of(ids, experts):
    tokens = ids.shape[1]
    expert = lax.broadcasted_iota(jnp.int32, (experts, tokens), 0)
    named = jnp.zeros((experts, tokens), F32)
    for k in range(ids.shape[0]):
        named = named + jnp.where(ids[k : k + 1, :] == expert, 1.0, 0.0)
    first = lax.broadcasted_iota(jnp.int32, (tokens, tokens), 0)
    second = lax.broadcasted_iota(jnp.int32, (tokens, tokens), 1)
    before = (first < second) & (first // ROWS == second // ROWS)
    rank = jnp.dot(
        named.astype(BF16), jnp.where(before, 1.0, 0.0).astype(BF16), preferred_element_type=F32
    )
    block = lax.broadcasted_iota(jnp.int32, (experts, tokens), 1) // ROWS
    return jnp.where(named > 0, rank + (block * CAP).astype(F32), -1.0)


def routing_kernel(ids, gates, slots, weights):
    experts, tokens = slots.shape
    slots[...] = slots_of(ids[...], experts)
    number = lax.broadcasted_iota(jnp.int32, (experts, tokens), 0)
    total = jnp.zeros((experts, tokens), F32)
    for k in range(ids.shape[0]):
        total = total + jnp.where(ids[k : k + 1, :] == number, gates[k : k + 1, :], 0.0)
    weights[...] = total


def route(ids, gates, experts):
    shape = jax.ShapeDtypeStruct((experts, ids.shape[1]), F32)
    return pl.pallas_call(
        routing_kernel,
        out_shape=(shape, shape),
        compiler_params=pltpu.CompilerParams(vmem_limit_bytes=16 << 20),
        name="routing",
    )(ids, gates)


def expert_kernel(rows, gate_w, up_w, down_w, out, gate, up, squares, act):
    step = pl.program_id(0)
    groups, taken, slots, width = rows.shape[1:]
    count = groups * slots
    model_width = gate_w.shape[1] * FIRST

    @pl.when(step < FIRST)
    def _():
        block = jnp.concatenate(
            [rows[0, :, i].reshape(count, width) for i in range(taken)], axis=1
        )
        gate_part = jnp.dot(block, gate_w[0], preferred_element_type=F32)
        up_part = jnp.dot(block, up_w[0], preferred_element_type=F32)
        wide = block.astype(F32)
        wide = wide * wide
        total = wide[:, :HEAD]
        for i in range(1, taken * width // HEAD):
            total = total + wide[:, i * HEAD : (i + 1) * HEAD]

        @pl.when(step == 0)
        def _():
            gate[...] = gate_part
            up[...] = up_part
            squares[...] = total

        @pl.when(step > 0)
        def _():
            gate[...] += gate_part
            up[...] += up_part
            squares[...] += total

    @pl.when(step == FIRST - 1)
    def _():
        mean = jnp.sum(squares[...], axis=1, keepdims=True) / model_width
        factor = lax.rsqrt(mean + 1e-06)
        value = gate[...] * factor
        act[...] = (value / (1.0 + jnp.exp(-value)) * (up[...] * factor)).astype(BF16)

    @pl.when(step >= FIRST)
    def _():
        result = jnp.dot(act[...], down_w[0], preferred_element_type=F32).astype(BF16)
        for i in range(out.shape[2]):
            out[0, :, i] = result[:, i * width : (i + 1) * width].reshape(groups, slots, width)


def expert(rows, gate_w, up_w, down_w):
    high, groups, low, slots, width = rows.shape
    hidden_units = gate_w.shape[2]
    count = groups * slots
    taken, given = high * low // FIRST, high * low // SECOND

    def first(i):
        return jnp.minimum(i, FIRST - 1)

    def second(i):
        return jnp.maximum(i - FIRST, 0)

    def block_at(i, size):
        return (i * size // low, 0, lax.rem(i, low // size), 0, 0)

    weight_spec = pl.BlockSpec((1, taken * width, hidden_units), lambda i: (0, first(i), 0))
    return pl.pallas_call(
        expert_kernel,
        grid=(FIRST + SECOND,),
        in_specs=[
            pl.BlockSpec((1, groups, taken, slots, width), lambda i: block_at(first(i), taken)),
            weight_spec,
            weight_spec,
            pl.BlockSpec((1, hidden_units, given * width), lambda i: (0, 0, second(i))),
        ],
        out_specs=pl.BlockSpec(
            (1, groups, given, slots, width), lambda i: block_at(second(i), given)
        ),
        out_shape=jax.ShapeDtypeStruct(rows.shape, BF16),
        scratch_shapes=[
            pltpu.VMEM((count, hidden_units), F32),
            pltpu.VMEM((count, hidden_units), F32),
            pltpu.VMEM((count, HEAD), F32),
            pltpu.VMEM((count, hidden_units), BF16),
        ],
        compiler_params=pltpu.CompilerParams(vmem_limit_bytes=56 << 20),
        name="expert",
    )(rows, gate_w, up_w, down_w)


def combine_kernel(slots, weights, answers, hidden, out, accum):
    step = pl.program_id(0)
    tokens = hidden.shape[0]
    count = answers.shape[0]

    @pl.when(step == 0)
    def _():
        accum[...] = hidden[...].astype(F32)

    row = lax.broadcasted_iota(jnp.int32, (SLOTS, tokens), 0).astype(F32)
    mine, scale = slots[...], weights[...]
    picks = [
        jnp.where(mine[e : e + 1, :] == row, scale[e : e + 1, :], 0.0).astype(BF16)
        for e in range(count)
    ]
    total = accum[...] + lax.dot_general(
        jnp.concatenate(picks, axis=0),
        answers[...].reshape(count * SLOTS, answers.shape[2]),
        (((0,), (0,)), ((), ())),
        preferred_element_type=F32,
    )
    accum[...] = total

    @pl.when(step == pl.num_programs(0) - 1)
    def _():
        out[...] = total.astype(BF16)


def combine(slots, weights, answers, hidden):
    tokens, width = hidden.shape
    experts = answers.shape[0]
    count = 32
    return pl.pallas_call(
        combine_kernel,
        grid=(experts // count,),
        in_specs=[
            pl.BlockSpec((count, tokens), lambda i: (i, 0)),
            pl.BlockSpec((count, tokens), lambda i: (i, 0)),
            pl.BlockSpec((count, SLOTS, width), lambda i: (i, 0, 0)),
            pl.BlockSpec((tokens, width), lambda i: (0, 0)),
        ],
        out_specs=pl.BlockSpec((tokens, width), lambda i: (0, 0)),
        out_shape=jax.ShapeDtypeStruct((tokens, width), BF16),
        scratch_shapes=[pltpu.VMEM((tokens, width), F32)],
        compiler_params=pltpu.CompilerParams(vmem_limit_bytes=32 << 20),
        name="combine",
    )(slots, weights, answers, hidden)


def gather_row(rotated_keys, value_matrix):
    own = jnp.concatenate([rotated_keys, value_matrix], axis=1)
    row = [own] + [lax.ppermute(own, "x", rotated(4, k)) for k in range(1, 4)]
    return jnp.concatenate(row)


def shift_row(row, step):
    return lax.ppermute(row, ("zh", "y"), rotated(8, step))


def gather_kv(row, shifted):
    tokens = row.shape[0] // 4
    middle, oldest = shifted[:3], shifted[3]
    near = jnp.arange(1, 4, dtype=jnp.int32) <= lax.axis_index("x")
    picked = jnp.where(jnp.repeat(near, tokens)[:, None], row[tokens:], oldest[tokens:])
    mine = jnp.concatenate([row[:tokens], oldest[:tokens], picked] + middle)
    return mine, lax.ppermute(mine, "c", flipped(2, 1))


def key_tables(tokens):
    x, core = lax.axis_index("x"), lax.axis_index("c")
    slab = lax.axis_index(("zh", "y"))
    steps = jnp.arange(1, 4, dtype=jnp.int32)
    back = jnp.concatenate(
        [jnp.array([0, 4], jnp.int32), jnp.where(steps <= x, 0, 4), jnp.repeat(steps, 4)]
    )
    turn = jnp.array([0, 0, 1, 2, 3] + [0, 1, 2, 3] * 3, jnp.int32)
    begin = ((slab - back) % 8) * 8 + ((x - turn) % 4) * 2
    begin = begin[None, :] + (core ^ jnp.arange(2, dtype=jnp.int32))[:, None]
    pos = begin[:, :, None] * tokens + jnp.arange(tokens, dtype=jnp.int32)
    chunks = begin[:, 5:].reshape(6, 4)
    low = jnp.min(chunks, axis=1) * tokens
    high = jnp.max(chunks, axis=1) * tokens + tokens - 1
    return pos.reshape(2, 1, 17 * tokens), low, high


def query_tables(tokens, lengths):
    query_pos = lax.axis_index(("zh", "y", "x", "c")) * tokens + jnp.arange(tokens, dtype=jnp.int32)
    starts = jnp.cumsum(lengths) - lengths
    query_start = jnp.max(
        jnp.where(starts[None, :] <= query_pos[:, None], starts[None, :], 0), axis=1
    ).astype(jnp.int32)
    lim = jnp.stack([query_pos[0], query_pos[-1], query_start[0], query_start[-1]])
    return lim, query_pos[:, None], query_start[:, None]


def gather_attended(own, others):
    def both(block):
        return [block, lax.ppermute(block, "c", flipped(2, 1))]

    near = lax.ppermute(own, Z, flipped(4, 1))
    far = lax.ppermute(own, Z, flipped(4, 3))
    near, far, *others = lax.optimization_barrier((near, far, *others))
    cut = own.shape[0] // 2
    first = lax.ppermute(near[:cut], Z, flipped(4, 3))
    second = lax.ppermute(far[cut:], Z, flipped(4, 1))
    return both(own) + both(near) + both(far) + both(first) + both(second), others


def body(
    queries,
    rotated_keys,
    value_matrix,
    lengths,
    out_weight,
    residual,
    expert_ids,
    router_gates,
    gate_proj,
    up_proj,
    down_proj,
):
    tokens = queries.shape[0]
    own_rows, model_width = residual.shape
    experts = 2 * 4 * 4 * 2 * 2
    width = model_width // GROUP

    row = gather_row(rotated_keys, value_matrix)

    weight_rows = out_weight.shape[0]
    meta = jnp.concatenate([expert_ids.astype(BF16), router_gates.astype(BF16)], axis=1)
    meta = meta.reshape(-1, width)
    used = meta.shape[0]
    meta = jnp.pad(meta, ((0, 16 - used), (0, 0)))
    sent = jnp.concatenate(
        [
            out_weight.reshape(weight_rows, GROUP, width).transpose(1, 0, 2),
            residual.reshape(own_rows, GROUP, width).transpose(1, 0, 2),
            jnp.broadcast_to(meta[None], (GROUP, 16, width)),
        ],
        axis=1,
    )
    got = lax.all_to_all(sent, LINE, split_axis=0, concat_axis=0, tiled=True)
    tables = key_tables(tokens) + query_tables(tokens, lengths)
    got, before, third = lax.optimization_barrier((got, shift_row(row, 1), shift_row(row, 3)))
    half = row.shape[0] // 2
    second, rest, oldest = lax.optimization_barrier(
        (shift_row(before[:half], 1), shift_row(third[half:], -1), shift_row(row, 4))
    )
    kv, other = gather_kv(row, [before, jnp.concatenate([second, rest]), third, oldest])
    weight = lax.all_gather(got[:, :weight_rows], ("y", "x"), axis=0, tiled=True)
    weight = weight.reshape(4, 4, GROUP, weight_rows, width)
    line_residual = got[:, weight_rows : weight_rows + own_rows]
    meta = got[:, weight_rows + own_rows : weight_rows + own_rows + used]
    meta = meta.reshape(GROUP * own_rows, 16).T
    ids = meta[:8].astype(jnp.int32)
    gates = meta[8:].astype(F32)
    slots, weights = route(ids, gates, experts)

    attended = attend(queries, kv, other, *tables)

    zl, core, zh = lax.axis_index("zl"), lax.axis_index("c"), lax.axis_index("zh")
    halves = []
    for high_part in range(2):
        for c in range(2):
            for k in range(2):
                halves.append((high_part * 2 + c) * 2 + (zl ^ k))
    places = [(zh ^ h) * 2 + (core ^ c) for h in range(2) for c in range(2)]
    table = jnp.stack(halves + places).astype(jnp.int32)
    blocks, (line_residual, slots, weights) = gather_attended(
        attended, (line_residual, slots, weights)
    )
    hidden, outgoing = project(table, blocks, weight, line_residual, slots)
    incoming = lax.all_to_all(outgoing, AXES, split_axis=0, concat_axis=0, tiled=True)
    produced = expert(
        incoming.reshape(2, 16, 4, SLOTS, width), gate_proj, up_proj, down_proj
    ).reshape(experts, SLOTS, width)
    answers = lax.all_to_all(produced, AXES, split_axis=0, concat_axis=0, tiled=True)
    mixed = combine(slots, weights, answers, hidden)
    final = lax.all_to_all(
        mixed.reshape(GROUP, own_rows, width), LINE, split_axis=0, concat_axis=0, tiled=True
    )
    return final.transpose(1, 0, 2).reshape(own_rows, model_width)


def solution(mesh):
    fine = Mesh(mesh.devices.reshape(2, 4, 4, 2, 2), AXES)
    ctx = ("zh", "y", "x", "c")
    both = P(AXES, None)
    in_specs = (
        P(ctx, "zl"),
        P(ctx, "zl"),
        P(ctx, "zl"),
        P(),
        P(("zl",) + ctx, None),
        both,
        both,
        both,
        P(AXES, None, None),
        P(AXES, None, None),
        P(AXES, None, None),
    )
    return jax.shard_map(body, mesh=fine, in_specs=in_specs, out_specs=both, check_vma=False)
```

```python
import functools
import math

import jax
import jax.numpy as jnp
from jax import lax
from jax.experimental import pallas as pl
from jax.experimental.pallas import tpu as pltpu
from jax.sharding import Mesh
from jax.sharding import PartitionSpec as P

HEAD = 128
CAP = 6
ROWS = 64
GROUP = 8
SLOTS = GROUP * CAP
CHUNK = 512
EDGE = 640
FIRST, SECOND = 4, 2
NEG = -1e30
BF16 = jnp.bfloat16
F32 = jnp.float32
AXES = ("zh", "y", "x", "c", "zl")
LINE = ("zh", "c", "zl")
Z = ("zh", "zl")


def rotated(count, step):
    return [(i, (i + step) % count) for i in range(count)]


def flipped(count, bits):
    return [(i, i ^ bits) for i in range(count)]


def attention_kernel(lim, low, high, q, kv, other, kpos, qpos, qstart, out, best, accum):
    scale = math.log2(math.e) / math.sqrt(HEAD)
    heads = q.shape[1] // HEAD
    tokens = q.shape[0]
    best[...] = jnp.full(best.shape, NEG, F32)
    accum[...] = jnp.zeros(accum.shape, F32)

    def update(source, begin, count, allowed):
        keys = source[pl.ds(begin, count), :HEAD]
        values = source[pl.ds(begin, count), HEAD:]
        values = jnp.concatenate([values, jnp.ones((count, HEAD), BF16)], axis=1)
        for head in range(heads):
            rows = pl.ds(head * tokens, tokens)
            scores = lax.dot_general(
                q[:, head * HEAD : (head + 1) * HEAD],
                keys,
                (((1,), (1,)), ((), ())),
                preferred_element_type=F32,
            )
            if allowed is not None:
                scores = jnp.where(allowed, scores, NEG)
            old = best[rows, :]
            new = jnp.maximum(old, jnp.max(scores, axis=1, keepdims=True))
            factor = jnp.exp2((old - new) * scale)
            expo = jnp.exp2((scores - jnp.concatenate([new] * (count // HEAD), axis=1)) * scale)
            added = jnp.dot(expo.astype(BF16), values, preferred_element_type=F32)
            accum[rows, :] = accum[rows, :] * jnp.concatenate([factor, factor], axis=1) + added
            best[rows, :] = new

    def inside(at):
        return (at <= qpos[...]) & (at >= qstart[...])

    for side, source in enumerate((kv, other)):
        update(source, 0, EDGE, inside(kpos[side, :, :EDGE]))

    full = (kv.shape[0] - EDGE) // CHUNK
    for side, source in enumerate((kv, other)):

        def step(i, carry, side=side, source=source):
            number = side * full + i
            used = (low[number] <= lim[1]) & (high[number] >= lim[2])
            whole = (high[number] <= lim[0]) & (low[number] >= lim[3])
            begin = pl.multiple_of(EDGE + i * CHUNK, HEAD)

            @pl.when(used & whole)
            def _():
                update(source, begin, CHUNK, None)

            @pl.when(used & jnp.logical_not(whole))
            def _():
                at = kpos[side, :, pl.ds(begin, CHUNK)]
                update(source, begin, CHUNK, inside(at))

            return carry

        lax.fori_loop(0, full, step, 0)

    for head in range(heads):
        rows = pl.ds(head * tokens, tokens)
        state = accum[rows, :]
        out[:, head * HEAD : (head + 1) * HEAD] = (state[:, :HEAD] / state[:, HEAD:]).astype(BF16)


def attend(queries, kv, other, key_pos, low, high, lim, query_pos, query_start):
    tokens, width = queries.shape
    smem = pl.BlockSpec(memory_space=pltpu.SMEM)
    vmem = pl.BlockSpec(memory_space=pltpu.VMEM)
    rows = width // HEAD * tokens
    return pl.pallas_call(
        attention_kernel,
        in_specs=[smem] * 3 + [vmem] * 6,
        out_specs=vmem,
        out_shape=jax.ShapeDtypeStruct((tokens, width), BF16),
        scratch_shapes=[pltpu.VMEM((rows, HEAD), F32), pltpu.VMEM((rows, 2 * HEAD), F32)],
        compiler_params=pltpu.CompilerParams(vmem_limit_bytes=32 << 20),
        cost_estimate=pl.CostEstimate(
            flops=10_000_000_000, bytes_accessed=4_000_000, transcendentals=8_000_000
        ),
        name="attention",
    )(lim, low, high, queries, kv, other, key_pos, query_pos, query_start)


def projection_kernel(steps, *refs):
    slot = refs[0]
    weight, residual, slots, hidden, outgoing, accum = refs[21:]
    step = pl.program_id(0)
    blocks, rows_each, width = residual.shape
    tokens = blocks * rows_each
    count = outgoing.shape[0]

    @pl.when(step < steps)
    def _():
        total = None
        for high in range(2):
            own, own_c, near, near_c, far, far_c, first, first_c, second, second_c = refs[
                1 + high : 21 : 2
            ]
            rows = ((own, own_c, first, second, first_c, second_c), (near, near_c, far, far_c))
            for other in range(2):
                pieces = []
                for x in range(4):
                    for core in range(2):
                        pieces.append(weight[0, x, slot[(high * 2 + core) * 2 + other]])
                part = jnp.dot(
                    jnp.concatenate([ref[...] for ref in rows[other]], axis=0),
                    jnp.concatenate(pieces, axis=0),
                    preferred_element_type=F32,
                )
                total = part if total is None else total + part

        @pl.when(step == 0)
        def _():
            accum[...] = total

        @pl.when(step > 0)
        def _():
            accum[...] += total

    @pl.when(step == steps - 1)
    def _():
        share = tokens // 4
        for block in range(4):
            place = slot[8 + block]
            part = accum[block * share : (block + 1) * share, :]
            base = jnp.concatenate([residual[2 * place], residual[2 * place + 1]], axis=0)
            here = pl.ds(pl.multiple_of(place * share, share), share)
            hidden[here, :] = (base.astype(F32) + part).astype(BF16)

    @pl.when(step >= steps)
    def _():
        row = lax.broadcasted_iota(jnp.int32, (SLOTS, tokens), 0).astype(F32)
        mine = slots[...]
        picks = [jnp.where(mine[e : e + 1, :] == row, 1.0, 0.0).astype(BF16) for e in range(count)]
        sent = jnp.dot(jnp.concatenate(picks, axis=0), hidden[...], preferred_element_type=F32)
        outgoing[...] = sent.astype(BF16).reshape(outgoing.shape)


def project(slot, blocks, weight, residual, slots):
    width = residual.shape[2]
    tokens = residual.shape[0] * residual.shape[1]
    experts = slots.shape[0]
    count = 16
    steps = weight.shape[0]
    depth = blocks[0].shape[1] // (2 * steps)

    def early(k):
        return jnp.minimum(k, steps - 1)

    def late(k):
        return jnp.maximum(k - steps, 0)

    specs = []
    for ref in blocks:
        specs.append(pl.BlockSpec((ref.shape[0], depth), lambda k: (0, early(k))))
        specs.append(pl.BlockSpec((ref.shape[0], depth), lambda k: (0, early(k) + steps)))
    return pl.pallas_call(
        functools.partial(projection_kernel, steps),
        grid=(steps + experts // count,),
        in_specs=[pl.BlockSpec(memory_space=pltpu.SMEM)]
        + specs
        + [
            pl.BlockSpec((1,) + weight.shape[1:], lambda k: (early(k), 0, 0, 0, 0)),
            pl.BlockSpec(residual.shape, lambda k: (0, 0, 0)),
            pl.BlockSpec((count, tokens), lambda k: (late(k), 0)),
        ],
        out_specs=(
            pl.BlockSpec((tokens, width), lambda k: (0, 0)),
            pl.BlockSpec((count, SLOTS, width), lambda k: (late(k), 0, 0)),
        ),
        out_shape=(
            jax.ShapeDtypeStruct((tokens, width), BF16),
            jax.ShapeDtypeStruct((experts, SLOTS, width), BF16),
        ),
        scratch_shapes=[pltpu.VMEM((tokens, width), F32)],
        compiler_params=pltpu.CompilerParams(vmem_limit_bytes=36 << 20),
        name="projection",
    )(slot, *[ref for ref in blocks for _ in range(2)], weight, residual, slots)


def slots_of(ids, experts):
    tokens = ids.shape[1]
    expert = lax.broadcasted_iota(jnp.int32, (experts, tokens), 0)
    named = jnp.zeros((experts, tokens), F32)
    for k in range(ids.shape[0]):
        named = named + jnp.where(ids[k : k + 1, :] == expert, 1.0, 0.0)
    first = lax.broadcasted_iota(jnp.int32, (tokens, tokens), 0)
    second = lax.broadcasted_iota(jnp.int32, (tokens, tokens), 1)
    before = (first < second) & (first // ROWS == second // ROWS)
    rank = jnp.dot(
        named.astype(BF16), jnp.where(before, 1.0, 0.0).astype(BF16), preferred_element_type=F32
    )
    block = lax.broadcasted_iota(jnp.int32, (experts, tokens), 1) // ROWS
    return jnp.where(named > 0, rank + (block * CAP).astype(F32), -1.0)


def routing_kernel(ids, gates, slots, weights):
    experts, tokens = slots.shape
    slots[...] = slots_of(ids[...], experts)
    number = lax.broadcasted_iota(jnp.int32, (experts, tokens), 0)
    total = jnp.zeros((experts, tokens), F32)
    for k in range(ids.shape[0]):
        total = total + jnp.where(ids[k : k + 1, :] == number, gates[k : k + 1, :], 0.0)
    weights[...] = total


def route(ids, gates, experts):
    shape = jax.ShapeDtypeStruct((experts, ids.shape[1]), F32)
    return pl.pallas_call(
        routing_kernel,
        out_shape=(shape, shape),
        compiler_params=pltpu.CompilerParams(vmem_limit_bytes=16 << 20),
        name="routing",
    )(ids, gates)


def expert_kernel(rows, gate_w, up_w, down_w, out, gate, up, squares, act):
    step = pl.program_id(0)
    groups, taken, slots, width = rows.shape[1:]
    count = groups * slots
    model_width = gate_w.shape[1] * FIRST

    @pl.when(step < FIRST)
    def _():
        block = jnp.concatenate(
            [rows[0, :, i].reshape(count, width) for i in range(taken)], axis=1
        )
        gate_part = jnp.dot(block, gate_w[0], preferred_element_type=F32)
        up_part = jnp.dot(block, up_w[0], preferred_element_type=F32)
        wide = block.astype(F32)
        wide = wide * wide
        total = wide[:, :HEAD]
        for i in range(1, taken * width // HEAD):
            total = total + wide[:, i * HEAD : (i + 1) * HEAD]

        @pl.when(step == 0)
        def _():
            gate[...] = gate_part
            up[...] = up_part
            squares[...] = total

        @pl.when(step > 0)
        def _():
            gate[...] += gate_part
            up[...] += up_part
            squares[...] += total

    @pl.when(step == FIRST - 1)
    def _():
        mean = jnp.sum(squares[...], axis=1, keepdims=True) / model_width
        factor = lax.rsqrt(mean + 1e-06)
        value = gate[...] * factor
        act[...] = (value / (1.0 + jnp.exp(-value)) * (up[...] * factor)).astype(BF16)

    @pl.when(step >= FIRST)
    def _():
        result = jnp.dot(act[...], down_w[0], preferred_element_type=F32).astype(BF16)
        for i in range(out.shape[2]):
            out[0, :, i] = result[:, i * width : (i + 1) * width].reshape(groups, slots, width)


def expert(rows, gate_w, up_w, down_w):
    high, groups, low, slots, width = rows.shape
    hidden_units = gate_w.shape[2]
    count = groups * slots
    taken, given = high * low // FIRST, high * low // SECOND

    def first(i):
        return jnp.minimum(i, FIRST - 1)

    def second(i):
        return jnp.maximum(i - FIRST, 0)

    def block_at(i, size):
        return (i * size // low, 0, lax.rem(i, low // size), 0, 0)

    weight_spec = pl.BlockSpec((1, taken * width, hidden_units), lambda i: (0, first(i), 0))
    return pl.pallas_call(
        expert_kernel,
        grid=(FIRST + SECOND,),
        in_specs=[
            pl.BlockSpec((1, groups, taken, slots, width), lambda i: block_at(first(i), taken)),
            weight_spec,
            weight_spec,
            pl.BlockSpec((1, hidden_units, given * width), lambda i: (0, 0, second(i))),
        ],
        out_specs=pl.BlockSpec(
            (1, groups, given, slots, width), lambda i: block_at(second(i), given)
        ),
        out_shape=jax.ShapeDtypeStruct(rows.shape, BF16),
        scratch_shapes=[
            pltpu.VMEM((count, hidden_units), F32),
            pltpu.VMEM((count, hidden_units), F32),
            pltpu.VMEM((count, HEAD), F32),
            pltpu.VMEM((count, hidden_units), BF16),
        ],
        compiler_params=pltpu.CompilerParams(vmem_limit_bytes=56 << 20),
        name="expert",
    )(rows, gate_w, up_w, down_w)


def combine_kernel(slots, weights, answers, hidden, out, accum):
    step = pl.program_id(0)
    tokens = hidden.shape[0]
    count = answers.shape[0]

    @pl.when(step == 0)
    def _():
        accum[...] = hidden[...].astype(F32)

    row = lax.broadcasted_iota(jnp.int32, (SLOTS, tokens), 0).astype(F32)
    mine, scale = slots[...], weights[...]
    picks = [
        jnp.where(mine[e : e + 1, :] == row, scale[e : e + 1, :], 0.0).astype(BF16)
        for e in range(count)
    ]
    total = accum[...] + lax.dot_general(
        jnp.concatenate(picks, axis=0),
        answers[...].reshape(count * SLOTS, answers.shape[2]),
        (((0,), (0,)), ((), ())),
        preferred_element_type=F32,
    )
    accum[...] = total

    @pl.when(step == pl.num_programs(0) - 1)
    def _():
        out[...] = total.astype(BF16)


def combine(slots, weights, answers, hidden):
    tokens, width = hidden.shape
    experts = answers.shape[0]
    count = 32
    return pl.pallas_call(
        combine_kernel,
        grid=(experts // count,),
        in_specs=[
            pl.BlockSpec((count, tokens), lambda i: (i, 0)),
            pl.BlockSpec((count, tokens), lambda i: (i, 0)),
            pl.BlockSpec((count, SLOTS, width), lambda i: (i, 0, 0)),
            pl.BlockSpec((tokens, width), lambda i: (0, 0)),
        ],
        out_specs=pl.BlockSpec((tokens, width), lambda i: (0, 0)),
        out_shape=jax.ShapeDtypeStruct((tokens, width), BF16),
        scratch_shapes=[pltpu.VMEM((tokens, width), F32)],
        compiler_params=pltpu.CompilerParams(vmem_limit_bytes=32 << 20),
        name="combine",
    )(slots, weights, answers, hidden)


def gather_row(rotated_keys, value_matrix):
    own = jnp.concatenate([rotated_keys, value_matrix], axis=1)
    row = [own] + [lax.ppermute(own, "x", rotated(4, k)) for k in range(1, 4)]
    return jnp.concatenate(row)


def shift_row(row, step):
    return lax.ppermute(row, ("zh", "y"), rotated(8, step))


def gather_kv(row, shifted):
    tokens = row.shape[0] // 4
    middle, oldest = shifted[:3], shifted[3]
    near = jnp.arange(1, 4, dtype=jnp.int32) <= lax.axis_index("x")
    picked = jnp.where(jnp.repeat(near, tokens)[:, None], row[tokens:], oldest[tokens:])
    mine = jnp.concatenate([row[:tokens], oldest[:tokens], picked] + middle)
    return mine, lax.ppermute(mine, "c", flipped(2, 1))


def key_tables(tokens):
    x, core = lax.axis_index("x"), lax.axis_index("c")
    slab = lax.axis_index(("zh", "y"))
    steps = jnp.arange(1, 4, dtype=jnp.int32)
    back = jnp.concatenate(
        [jnp.array([0, 4], jnp.int32), jnp.where(steps <= x, 0, 4), jnp.repeat(steps, 4)]
    )
    turn = jnp.array([0, 0, 1, 2, 3] + [0, 1, 2, 3] * 3, jnp.int32)
    begin = ((slab - back) % 8) * 8 + ((x - turn) % 4) * 2
    begin = begin[None, :] + (core ^ jnp.arange(2, dtype=jnp.int32))[:, None]
    pos = begin[:, :, None] * tokens + jnp.arange(tokens, dtype=jnp.int32)
    chunks = begin[:, 5:].reshape(6, 4)
    low = jnp.min(chunks, axis=1) * tokens
    high = jnp.max(chunks, axis=1) * tokens + tokens - 1
    return pos.reshape(2, 1, 17 * tokens), low, high


def query_tables(tokens, lengths):
    query_pos = lax.axis_index(("zh", "y", "x", "c")) * tokens + jnp.arange(tokens, dtype=jnp.int32)
    starts = jnp.cumsum(lengths) - lengths
    query_start = jnp.max(
        jnp.where(starts[None, :] <= query_pos[:, None], starts[None, :], 0), axis=1
    ).astype(jnp.int32)
    lim = jnp.stack([query_pos[0], query_pos[-1], query_start[0], query_start[-1]])
    return lim, query_pos[:, None], query_start[:, None]


def gather_attended(own, others):
    def both(block):
        return [block, lax.ppermute(block, "c", flipped(2, 1))]

    near = lax.ppermute(own, Z, flipped(4, 1))
    far = lax.ppermute(own, Z, flipped(4, 3))
    near, far, *others = lax.optimization_barrier((near, far, *others))
    cut = own.shape[0] // 2
    first = lax.ppermute(near[:cut], Z, flipped(4, 3))
    second = lax.ppermute(far[cut:], Z, flipped(4, 1))
    return both(own) + both(near) + both(far) + both(first) + both(second), others


def body(
    queries,
    rotated_keys,
    value_matrix,
    lengths,
    out_weight,
    residual,
    expert_ids,
    router_gates,
    gate_proj,
    up_proj,
    down_proj,
):
    tokens = queries.shape[0]
    own_rows, model_width = residual.shape
    experts = 2 * 4 * 4 * 2 * 2
    width = model_width // GROUP

    row = gather_row(rotated_keys, value_matrix)

    weight_rows = out_weight.shape[0]
    meta = jnp.concatenate([expert_ids.astype(BF16), router_gates.astype(BF16)], axis=1)
    meta = meta.reshape(-1, width)
    used = meta.shape[0]
    meta = jnp.pad(meta, ((0, 16 - used), (0, 0)))
    sent = jnp.concatenate(
        [
            out_weight.reshape(weight_rows, GROUP, width).transpose(1, 0, 2),
            residual.reshape(own_rows, GROUP, width).transpose(1, 0, 2),
            jnp.broadcast_to(meta[None], (GROUP, 16, width)),
        ],
        axis=1,
    )
    got = lax.all_to_all(sent, LINE, split_axis=0, concat_axis=0, tiled=True)
    tables = key_tables(tokens) + query_tables(tokens, lengths)
    got, before, third = lax.optimization_barrier((got, shift_row(row, 1), shift_row(row, 3)))
    half = row.shape[0] // 2
    second, rest, oldest, *tables = lax.optimization_barrier(
        (shift_row(before[:half], 1), shift_row(third[half:], -1), shift_row(row, 4)) + tables
    )
    kv, other = gather_kv(row, [before, jnp.concatenate([second, rest]), third, oldest])
    weight = lax.all_gather(got[:, :weight_rows], ("y", "x"), axis=0, tiled=True)
    weight = weight.reshape(4, 4, GROUP, weight_rows, width)
    line_residual = got[:, weight_rows : weight_rows + own_rows]
    meta = got[:, weight_rows + own_rows : weight_rows + own_rows + used]
    meta = meta.reshape(GROUP * own_rows, 16).T
    ids = meta[:8].astype(jnp.int32)
    gates = meta[8:].astype(F32)
    slots, weights = route(ids, gates, experts)

    attended = attend(queries, kv, other, *tables)

    zl, core, zh = lax.axis_index("zl"), lax.axis_index("c"), lax.axis_index("zh")
    halves = []
    for high_part in range(2):
        for c in range(2):
            for k in range(2):
                halves.append((high_part * 2 + c) * 2 + (zl ^ k))
    places = [(zh ^ h) * 2 + (core ^ c) for h in range(2) for c in range(2)]
    table = jnp.stack(halves + places).astype(jnp.int32)
    blocks, (line_residual, slots, weights) = gather_attended(
        attended, (line_residual, slots, weights)
    )
    hidden, outgoing = project(table, blocks, weight, line_residual, slots)
    incoming = lax.all_to_all(outgoing, AXES, split_axis=0, concat_axis=0, tiled=True)
    produced = expert(
        incoming.reshape(2, 16, 4, SLOTS, width), gate_proj, up_proj, down_proj
    ).reshape(experts, SLOTS, width)
    answers = lax.all_to_all(produced, AXES, split_axis=0, concat_axis=0, tiled=True)
    mixed = combine(slots, weights, answers, hidden)
    final = lax.all_to_all(
        mixed.reshape(GROUP, own_rows, width), LINE, split_axis=0, concat_axis=0, tiled=True
    )
    return final.transpose(1, 0, 2).reshape(own_rows, model_width)


def solution(mesh):
    fine = Mesh(mesh.devices.reshape(2, 4, 4, 2, 2), AXES)
    ctx = ("zh", "y", "x", "c")
    both = P(AXES, None)
    in_specs = (
        P(ctx, "zl"),
        P(ctx, "zl"),
        P(ctx, "zl"),
        P(),
        P(("zl",) + ctx, None),
        both,
        both,
        both,
        P(AXES, None, None),
        P(AXES, None, None),
        P(AXES, None, None),
    )
    return jax.shard_map(body, mesh=fine, in_specs=in_specs, out_specs=both, check_vma=False)
```
